32 devices in a mesh: dp: 16 (over z, y, x), tensor: 2 (over core).
Axes of the slice: x: 2, y: 2, z: 4, core: 2. Of those that a mesh axis runs over, the one named last changes fastest.
Arguments:
- tokens: bfloat16 [17024, 768], P('dp'), may hold values from -6 to 6
- counts: int32 [16, 2], P('dp'), may hold values from 0 to 2, as said below
- cotangent: bfloat16 [17024, 768], P('dp'), may hold values from -6 to 6
- ln1_gain: float32 [768], replicated, may hold values from 0.5 to 1.5
- ln1_bias: float32 [768], replicated, may hold values from -3 to 3
- qkv_weight: bfloat16 [768, 3, 768], P(None, None, 'tensor'), may hold values from -0.21875 to 0.21875
- qv_bias: float32 [2, 768], P(None, 'tensor'), may hold values from -3 to 3
- out_weight: bfloat16 [768, 768], P('tensor'), may hold values from -2 to 2
- out_bias: float32 [768], replicated, may hold values from -3 to 3
- ln2_gain: float32 [768], replicated, may hold values from 0.5 to 1.5
- ln2_bias: float32 [768], replicated, may hold values from -3 to 3
- up_weight: bfloat16 [768, 3072], P(None, 'tensor'), may hold values from -0.21875 to 0.21875
- up_bias: float32 [3072], P('tensor'), may hold values from -3 to 3
- down_weight: bfloat16 [3072, 768], P('tensor'), may hold values from -0.109375 to 0.109375
- down_bias: float32 [768], replicated, may hold values from -3 to 3
Outputs:
- output: bfloat16 [17024, 768], P('dp')
- input_grad: bfloat16 [17024, 768], P('dp')
- ln1_gain_grad: float32 [768], P('dp')
- ln1_bias_grad: float32 [768], P('dp')
- qkv_weight_grad: float32 [768, 3, 768], P('dp', None, 'tensor')
- qv_bias_grad: float32 [2, 768], P(None, 'tensor')
- out_weight_grad: float32 [768, 768], P('tensor', 'dp')
- out_bias_grad: float32 [768], P('dp')
- ln2_gain_grad: float32 [768], P('dp')
- ln2_bias_grad: float32 [768], P('dp')
- up_weight_grad: float32 [768, 3072], P('dp', 'tensor')
- up_bias_grad: float32 [3072], P('tensor')
- down_weight_grad: float32 [3072, 768], P('tensor', 'dp')
- down_bias_grad: float32 [768], P('dp')
The draws below stay inside these ranges and needn't reach their ends.
Inputs may be any that keep to these rules, and one draw needn't show every extreme that they name: counts[d, 0] counts live slots of 608 tokens (at most 1) and counts[d, 1] live slots of 228 tokens (at most 2) on dp device d; live slots come first in each kind; some device has all its slots live and some device has no live long slot.
All inputs are finite; a program needn't handle non-finite values.
Results may differ from the reference program's by a relative error of at most 0.0095.
Values sent between devices are 32-bit elements; how exact they have to be, the bound alone decides.
No kernel may reach another device: no remote copies, remote signals or barrier semaphores. Data moves between devices by JAX's collectives and lax.ppermute only.
A program may use at most 192 MiB of HBM per device.

```python
import jax
import jax.numpy as jnp
from jax import lax

D = 768
HEADS = 12
FF = 3072
HEAD_DIM = 64
LONG_LEN = 608
SHORT_LEN = 228
LONG_SLOTS = 1
SHORT_SLOTS = 2
TOKENS = 17024
N_DP = 16


def draw_counts(key, part):
    key = jax.random.fold_in(key, 11)
    streams = jax.random.split(key, 4)
    longs = jax.random.randint(streams[0], (N_DP,), 0, LONG_SLOTS + 1)
    shorts = jax.random.randint(streams[1], (N_DP,), 0, SHORT_SLOTS + 1)
    filled = jax.random.randint(streams[2], (), 0, N_DP)
    emptied = (filled + 1 + jax.random.randint(streams[3], (), 0, N_DP - 1)) % N_DP
    positions = jnp.arange(N_DP)
    longs = jnp.where(positions == filled, LONG_SLOTS, longs)
    shorts = jnp.where(positions == filled, SHORT_SLOTS, shorts)
    longs = jnp.where(positions == emptied, 0, longs)
    return jnp.stack([longs, shorts], axis=1).astype(jnp.int32)


def strengthened(drawn, rng, source, target, blocks, factor):
    def block_of(dim):
        return (jnp.arange(drawn.shape[dim]) // (drawn.shape[dim] // blocks)).reshape((-1,) + (1,) * (drawn.ndim - 1 - dim))

    near = jax.random.permutation(rng, blocks)[block_of(target)]
    second = (block_of(target) + blocks // 2) % blocks
    return jnp.where((block_of(source) == near) | (block_of(source) == second), factor * drawn, drawn)


def level_of(own_key, extent, shards, smallest, top_value):
    loudness = 1.0
    for dim, parts in shards:
        heights = jax.random.uniform(jax.random.fold_in(jax.random.fold_in(own_key, 6), dim), (parts,), jnp.float32, smallest / len(shards), top_value / len(shards))
        loudness = loudness * jnp.repeat(jnp.exp(heights), extent[dim] // parts).reshape((-1,) + (1,) * (len(extent) - 1 - dim))
    return loudness


def scatter_about(stream_key, extent, scale, limit, cuts=(), dtype=jnp.bfloat16):
    loudness = level_of(stream_key, extent, cuts, -0.22, 0.18) if cuts else 1.0
    values = jax.random.normal(stream_key, extent, jnp.float32) * scale * loudness
    return jnp.minimum(jnp.maximum(values, -limit), limit).astype(dtype)


def noise_with(key, dims, deviation, bound, cuts, heavy, held_as=jnp.bfloat16):
    drawn = deviation * jax.random.normal(key, dims, jnp.float32)
    if cuts:
        drawn = drawn * level_of(key, dims, cuts, -0.22, 0.18)
    return jnp.clip(strengthened(drawn, jax.random.fold_in(key, 3), *heavy), -bound, bound).astype(held_as)


def setup_inputs(seed: int = 0) -> dict:
    key_of = jax.random.split(jax.random.key(seed), 16)
    return {
        "tokens": noise_with(key_of[0], (TOKENS, D), 1.0, 6.0, ((0, 16),), (0, 1, 16, 2.0)),
        "counts": draw_counts(jax.random.fold_in(key_of[15], 71), 0),
        "cotangent": noise_with(key_of[2], (TOKENS, D), 1.0, 6.0, ((0, 16),), (0, 1, 16, 2.0)),
        "ln1_gain": jnp.clip(1.0 + 0.1 * jax.random.normal(key_of[3], (D,), jnp.float32), 0.5, 1.5),
        "ln1_bias": scatter_about(key_of[4], (D,), 0.5, 3.0, (), jnp.float32),
        "qkv_weight": scatter_about(key_of[5], (D, 3, D), D ** -0.5, 0.21875, ((2, 2),)),
        "qv_bias": scatter_about(key_of[6], (2, D), 0.5, 3.0, ((1, 2),), jnp.float32),
        "out_weight": scatter_about(key_of[7], (D, D), (8 * D // LONG_LEN) ** -0.5, 2.0, ((0, 2),)),
        "out_bias": scatter_about(key_of[8], (D,), 0.5, 3.0, (), jnp.float32),
        "ln2_gain": jnp.clip(1.0 + 0.1 * jax.random.normal(key_of[9], (D,), jnp.float32), 0.5, 1.5),
        "ln2_bias": scatter_about(key_of[10], (D,), 0.5, 3.0, (), jnp.float32),
        "up_weight": scatter_about(key_of[11], (D, FF), D ** -0.5, 0.21875, ((1, 2),)),
        "up_bias": scatter_about(key_of[12], (FF,), 0.5, 3.0, ((0, 2),), jnp.float32),
        "down_weight": scatter_about(key_of[13], (FF, D), FF ** -0.5, 0.109375, ((0, 2),)),
        "down_bias": scatter_about(key_of[14], (D,), 0.5, 3.0, (), jnp.float32),
    }


EPS = 1e-06

@jax.custom_vjp
def low(v):
    return lax.optimization_barrier(v.astype(jnp.bfloat16)).astype(jnp.float32)

@jax.custom_vjp
def low_back(v):
    return v

def low_keep(v):
    return (low(v), None)

def low_pass(kept, grad):
    return (grad,)

def back_keep(v):
    return (v, None)

def back_low(kept, grad):
    return (low(grad),)
low.defvjp(low_keep, low_pass)
low_back.defvjp(back_keep, back_low)

def dense(left, right):
    return jnp.dot(left, right, precision=lax.Precision.HIGHEST)

def normalize(values, gain, shift):
    center = values - lax.optimization_barrier(jnp.mean(values, axis=-1, keepdims=True))
    spread = lax.optimization_barrier(jnp.mean(center * center, axis=-1, keepdims=True))
    return center * lax.rsqrt(spread + EPS) * gain + shift

def rounded(values):
    return low_back(low(values))

def live_rows(count_row):
    long_slot = jnp.arange(LONG_SLOTS * LONG_LEN) // LONG_LEN
    short_slot = jnp.arange(SHORT_SLOTS * SHORT_LEN) // SHORT_LEN
    return jnp.concatenate([long_slot < count_row[0], short_slot < count_row[1]]).astype(jnp.float32)

def attend(query, key_rows, value_rows, length):
    number = query.shape[0] // length
    shape = (number, length, HEADS, HEAD_DIM)
    scores = jnp.einsum('slhd,smhd->shlm', query.reshape(shape), key_rows.reshape(shape), precision=lax.Precision.HIGHEST)
    scores = low_back(scores)
    probs = low(jax.nn.softmax(scores, axis=-1))
    mixed = jnp.einsum('shlm,smhd->slhd', probs, value_rows.reshape(shape), precision=lax.Precision.HIGHEST)
    return mixed.reshape(number * length, D)

def layer(weights, inputs, live):
    gain_one, shift_one, qkv_mat, qv_add, out_mat, out_add, gain_two, shift_two, up_mat, up_add, down_mat, down_add = weights
    scale = HEAD_DIM ** (-0.5)
    normed = low(normalize(inputs, gain_one, shift_one))
    projected = dense(normed, qkv_mat.reshape(D, 3 * D)).reshape(-1, 3, D)
    query = rounded((projected[:, 0] + qv_add[0]) * scale)
    key_rows = rounded(projected[:, 1])
    value_rows = rounded(projected[:, 2] + qv_add[1])
    split = LONG_SLOTS * LONG_LEN
    mixed = jnp.concatenate([attend(query[:split], key_rows[:split], value_rows[:split], LONG_LEN), attend(query[split:], key_rows[split:], value_rows[split:], SHORT_LEN)])
    mixed = rounded(mixed)
    attended = low_back(dense(mixed, out_mat) + out_add)
    middle = inputs + attended
    normed_two = low(normalize(middle, gain_two, shift_two))
    hidden = low_back(dense(normed_two, up_mat) + up_add)
    activated = low(jax.nn.gelu(hidden, approximate=False))
    produced = low_back(dense(activated, down_mat) + down_add)
    return live[:, None] * (middle + produced)

def reference(tokens, counts, cotangent, ln1_gain, ln1_bias, qkv_weight, qv_bias, out_weight, out_bias, ln2_gain, ln2_bias, up_weight, up_bias, down_weight, down_bias):
    params = tuple((item.astype(jnp.float32) for item in (ln1_gain, ln1_bias, qkv_weight, qv_bias, out_weight, out_bias, ln2_gain, ln2_bias, up_weight, up_bias, down_weight, down_bias)))
    rows = LONG_SLOTS * LONG_LEN + SHORT_SLOTS * SHORT_LEN
    inputs = tokens.astype(jnp.float32).reshape(N_DP, rows, D)
    lives = jax.vmap(live_rows)(counts)

    def forward(weights, stacked):

        def single(pair):
            return layer(weights, pair[0], pair[1])
        return lax.map(jax.checkpoint(single), (stacked, lives))
    result, pullback = jax.vjp(forward, params, inputs)
    grad_params, grad_inputs = pullback(cotangent.astype(jnp.float32).reshape(N_DP, rows, D))
    output = result.reshape(N_DP * rows, D).astype(jnp.bfloat16)
    input_grad = grad_inputs.reshape(N_DP * rows, D).astype(jnp.bfloat16)
    g_one, s_one, g_qkv, g_qv, g_out, g_outb, g_two, s_two, g_up, g_upb, g_down, g_downb = grad_params
    return (output, input_grad, g_one, s_one, g_qkv, g_qv, g_out, g_outb, g_two, s_two, g_up, g_upb, g_down, g_downb)
```

```python
import functools
import math

import jax
import jax.numpy as jnp
from jax import lax
from jax.experimental import pallas as pl
from jax.experimental.pallas import tpu as pltpu
from jax.sharding import PartitionSpec as P

HEAD_DIM = 64
LONG_LEN = 608
SHORT_LEN = 228
LONG_SLOTS = 1
SHORT_SLOTS = 2
EPS = 1e-06

LANES = 128
PAIR = 2 * HEAD_DIM
BF = jnp.bfloat16
F32 = jnp.float32
VMEM_LIMIT = 60 * 1024 * 1024


def up_to(value, unit):
    return -(-value // unit) * unit


def slots():
    found, src, dst = [], 0, 0
    for kind, (number, length) in enumerate(((LONG_SLOTS, LONG_LEN), (SHORT_SLOTS, SHORT_LEN))):
        for index in range(number):
            room = up_to(length, LANES)
            found.append((src, length, dst, room, kind, index))
            src, dst = src + length, dst + room
    return found, src, dst


SLOTS, ROWS, PADDED = slots()
SPLIT = sum(slot[3] for slot in SLOTS if slot[4] == 0)
CHUNK = PADDED // 3


def row(ref):
    return ref[...].reshape(1, -1)


def nn(left, right):
    return lax.dot_general(left, right, (((1,), (0,)), ((), ())), preferred_element_type=F32)


def nt(left, right):
    return lax.dot_general(left, right, (((1,), (1,)), ((), ())), preferred_element_type=F32)


COSTS = {
    "down": 1000000000,
    "mlp_gda": 1000000000,
    "project_back_a": 5000000000,
    "turn_normed": 1000000000,
    "cotangent": 5000000000,
    "project_back_b": 1000000000,
    "mlp_gub": 1000000000,
    "mlp_gdb": 5000000000,
    "input_back": 5000000000,
    "attend": 5000000000,
}


def held(shape, dtype):
    shape = (1, *shape)
    lead = math.prod(shape[:-2])
    return lead * up_to(shape[-2], 16) * up_to(shape[-1], LANES) * jnp.dtype(dtype).itemsize


class Far:
    def __init__(self, value, chunks=1, rows=None, cols=None, wait=False):
        self.value, self.chunks, self.rows, self.cols, self.wait = value, chunks, rows, cols, wait

    @property
    def shape(self):
        shape = list(self.value.shape)
        if self.rows is not None:
            shape[0] = self.rows[1]
        if self.cols is not None:
            shape[-1] = self.cols[1]
        return tuple(shape)

    @property
    def dtype(self):
        return self.value.dtype


class Late:
    def __init__(self, spec, source, buffer, sems):
        self.buffer, self.left = buffer, {}
        if spec.rows is not None:
            source = source.at[pl.ds(*spec.rows)]
        if spec.cols is not None:
            source = source.at[..., pl.ds(*spec.cols)]
        size = spec.shape[0] // spec.chunks
        for i in range(spec.chunks):
            parts = (source, buffer)
            if spec.chunks > 1:
                parts = (ref.at[i * size : (i + 1) * size] for ref in parts)
            self.left[i] = pltpu.make_async_copy(*parts, sems.at[i])
        if not spec.wait:
            self.start()

    def start(self):
        for copy in self.left.values():
            copy.start()

    def rows(self, i):
        if i in self.left:
            self.left.pop(i).wait()
        return self.buffer

    def all(self):
        for i in list(self.left):
            self.rows(i)
        return self.buffer

    @property
    def shape(self):
        return self.buffer.shape

    def __getitem__(self, key):
        return self.all()[key]


def part_of(ref, i):
    rows = slice(i * LANES, (i + 1) * LANES)
    return ref.rows(i)[rows, :] if isinstance(ref, Late) else ref[rows, :]


class Away:
    def __init__(self, buffer, target, sems, chunks):
        self.buffer, self.target, self.sems, self.chunks, self.sent = buffer, target, sems, chunks, []

    @property
    def shape(self):
        return self.buffer.shape

    def __setitem__(self, key, value):
        self.buffer[key] = value

    def __getitem__(self, key):
        return self.buffer[key]

    def send(self, i=None):
        parts = (self.buffer, self.target)
        if i is not None:
            size = self.buffer.shape[0] // self.chunks
            parts = (ref.at[i * size : (i + 1) * size] for ref in parts)
        copy = pltpu.make_async_copy(*parts, self.sems.at[i or 0])
        copy.start()
        self.sent.append(copy)


def call(body, outs, args, scratch=(), smem=0, sems=0, name=None, room=4):
    specs = [pl.BlockSpec(memory_space=pltpu.SMEM)] * smem
    buffers = []
    for arg in args[smem:]:
        far = isinstance(arg, Far)
        specs.append(pl.BlockSpec(memory_space=pl.ANY if far else pltpu.VMEM))
        if far:
            if arg.chunks:
                buffers += [pltpu.VMEM(arg.shape, arg.dtype), pltpu.SemaphoreType.DMA((arg.chunks,))]
    for out in outs:
        if len(out) > 2 and out[2]:
            buffers += [pltpu.VMEM(out[0], out[1]), pltpu.SemaphoreType.DMA((out[2],))]
    need = sum(held(*item[:2]) for item in [*(out for out in outs if len(out) > 2 and out[2]), *scratch])
    need += sum(held(arg.shape, arg.dtype) for arg in args[smem:] if isinstance(arg, Far) and arg.chunks)
    spaces = [pltpu.SMEM] * smem + [pltpu.HBM if isinstance(arg, Far) else pltpu.VMEM for arg in args[smem:]]
    values = [arg.value if isinstance(arg, Far) else arg for arg in args]
    values[smem:] = [pltpu.with_memory_space_constraint(*pair) for pair in zip(values[smem:], spaces[smem:])]

    def run(*refs):
        given, refs = refs[: len(args)], refs[len(args) :]
        made, refs = refs[: len(outs)], refs[len(outs) :]
        count = len(scratch) + (1 if sems else 0)
        own, extra = refs[:count], list(refs[count:])
        ins, results = [], []
        for arg, ref in zip(args, given):
            late = isinstance(arg, Far) and arg.chunks
            ins.append(Late(arg, ref, extra.pop(0), extra.pop(0)) if late else ref)
        for out, ref in zip(outs, made):
            away = len(out) > 2 and out[2]
            results.append(Away(extra.pop(0), ref, extra.pop(0), out[2]) if away else ref)
        body(*ins, *results, *own)
        for item in ins:
            if isinstance(item, Late):
                item.all()
        for item in results:
            if isinstance(item, Away):
                for copy in item.sent:
                    copy.wait()

    return pl.pallas_call(
        run,
        out_shape=[pltpu.HBM(*out[:2]) if len(out) > 2 else pltpu.VMEM(*out) for out in outs],
        in_specs=specs,
        out_specs=[pl.BlockSpec(memory_space=pl.ANY if len(out) > 2 else pltpu.VMEM) for out in outs],
        scratch_shapes=[pltpu.VMEM(*item) for item in scratch]
        + ([pltpu.SemaphoreType.DMA((sems,))] if sems else [])
        + buffers,
        compiler_params=pltpu.CompilerParams(vmem_limit_bytes=need + room * 2**20),
        cost_estimate=pl.CostEstimate(flops=COSTS.get(name, 1000), bytes_accessed=1000, transcendentals=0),
        name=name,
    )(*values)


def row_loop(step, body, rows=PADDED):
    def run(i, carry):
        body(pl.ds(pl.multiple_of(i * step, step), step))
        return carry

    lax.fori_loop(0, rows // step, run, 0)


def normal_parts(values):
    center = values - jnp.mean(values, axis=-1, keepdims=True)
    spread = jnp.mean(center * center, axis=-1, keepdims=True)
    ratio = lax.rsqrt(spread + EPS)
    return center * ratio, ratio


def norm_back(values, gain, grad):
    hat, ratio = normal_parts(values)
    scaled = grad * gain
    mean_one = jnp.mean(scaled, axis=-1, keepdims=True)
    mean_two = jnp.mean(scaled * hat, axis=-1, keepdims=True)
    back = ratio * (scaled - mean_one - hat * mean_two)
    return back, jnp.sum(grad * hat, axis=0, keepdims=True), jnp.sum(grad, axis=0, keepdims=True)


def spread(source, wide, write):
    wide[:ROWS, :] = source[...].astype(F32)
    for slot in SLOTS:
        src, length, dst, room = slot[:4]
        for i in range(0, room, LANES):
            values = wide[src + i : src + i + LANES, :]
            if i + LANES > length:
                row = lax.broadcasted_iota(jnp.int32, values.shape, 0)
                values = jnp.where(row < length - i, values, 0.0)
            write(slice(dst + i, dst + i + LANES), values, slot)


def gather(read, wide, target):
    for slot in SLOTS:
        src, _, dst, room = slot[:4]
        for i in range(0, room, LANES):
            wide[src + i : src + i + LANES, :] = read(slice(dst + i, dst + i + LANES), slot)
    target[...] = wide[:ROWS, :].astype(target.dtype)


WIDE = up_to(ROWS + LANES, LANES)


def project_body(tokens, gain, shift, weight, bias, tok, normed, qkv, wide):
    width = weight.shape[2]
    scale = HEAD_DIM ** (-0.5)

    def write(rows, values, slot):
        tok[rows, :] = values.astype(BF)
        hat, _ = normal_parts(values)
        normed[rows, :] = (hat * row(gain) + row(shift)).astype(BF)

    spread(tokens, wide, write)
    qkv[:, :width] = ((nn(normed[...], weight[0]) + bias[0:1, :]) * scale).astype(BF)
    qkv[:, width : 2 * width] = nn(normed[...], weight[1]).astype(BF)
    qkv[:, 2 * width :] = (nn(normed[...], weight[2]) + bias[1:2, :]).astype(BF)
    qkv.send()


UNIT = 256


def head_mask(rows, which):
    lane = lax.broadcasted_iota(jnp.int32, (rows, PAIR), 1)
    return (lane // HEAD_DIM) == which


def both_heads(block):
    zero = jnp.zeros_like(block)
    return jnp.concatenate([jnp.where(head_mask(block.shape[0], which), block, zero) for which in range(2)])


def join_heads(block):
    half = block.shape[0] // 2
    return jnp.where(head_mask(half, 0), block[:half], block[half:])


def attend_body(plan, qkv, out_weight, mixed, lse, part):
    width = qkv.shape[1] // 3
    for start, length, room, local in plan:
        lane = lax.broadcasted_iota(jnp.int32, (room, LANES), 1)
        keep = lax.broadcasted_iota(jnp.int32, (1, room), 1) < length
        stats = jnp.zeros((room, LANES), F32)
        for pair in range(width // PAIR):
            q, k, v = (
                qkv[start : start + room, n * width + pair * PAIR : n * width + (pair + 1) * PAIR] for n in range(3)
            )
            scores = jnp.where(keep, nt(both_heads(q), k), -1e30)
            top = jnp.max(scores, axis=-1, keepdims=True)
            expo = jnp.exp(scores - top)
            total = jnp.sum(expo, axis=-1, keepdims=True)
            out = nn(expo.astype(BF), v) / total
            mixed[local : local + room, pair * PAIR : (pair + 1) * PAIR] = join_heads(out).astype(BF)
            log_total = top + jnp.log(total)
            stats = jnp.where(lane == 2 * pair, log_total[:room], stats)
            stats = jnp.where(lane == 2 * pair + 1, log_total[room:], stats)
        lse[local : local + room, :] = stats
    mixed.send()
    lse.send()
    part[...] = nn(mixed[...], out_weight[...])


def front_body(plan, me, tokens, gain, shift, weight, bias, out_weight, *refs):
    fetched, (tok, normed, tok_far), (qkv, mixed, lse, part, rest, kept) = refs[:3], refs[3:6], refs[6:12]
    targets, (wide, sems) = refs[12:15], refs[15:]
    copies = [pltpu.make_async_copy(*pair, sems.at[n]) for n, pair in enumerate(zip(fetched, targets))]
    copies.append(pltpu.make_async_copy(tok, tok_far, sems.at[len(copies)]))
    project_body(tokens, gain, shift, weight, bias, tok, normed, qkv, wide)
    out_weight.start()
    for copy in copies:
        copy.start()
    rest[...] = qkv[SPLIT:, :]
    attend_body(plan, qkv, out_weight, mixed, lse, part)
    kept[...] = out_weight[...]
    for copy in copies:
        copy.wait()


def hidden_body(tok, add, gain, shift, own_a, got_a, own_b, got_b, up, up_add, gd, down, middle, normed, act, gh, gh_sum):
    for i in range(PADDED // LANES):
        rows = slice(i * LANES, (i + 1) * LANES)
        base, own, got = (0, own_a, got_a) if i < SPLIT // LANES else (SPLIT, own_b, got_b)
        n = i - base // LANES
        mid = part_of(tok, i).astype(F32) + (part_of(own, n) + part_of(got, n) + row(add))
        middle[rows, :] = mid
        hat, _ = normal_parts(mid)
        normed[rows, :] = (hat * row(gain) + row(shift)).astype(BF)
    for start in range(0, PADDED, CHUNK):
        rows = slice(start, start + CHUNK)
        for col in range(0, act.shape[1], UNIT):
            cols = slice(col, col + UNIT)
            hidden = nn(normed[rows, :], up[:, cols]) + row(up_add)[:, cols]
            cdf = 0.5 + 0.5 * lax.erf(hidden * (2.0**-0.5))
            act[rows, cols] = (hidden * cdf).astype(BF)
            slope = cdf + hidden * (jnp.exp(hidden * hidden * -0.5) * ((2.0 * math.pi) ** -0.5))
            gh[rows, cols] = (nt(gd[rows, :], down[cols, :]) * slope).astype(BF)
    gh_sum[...] = jnp.sum(gh[...].astype(F32), axis=0, keepdims=True)


def transpose_body(source, target):
    source = source.all() if isinstance(source, Late) else source
    def step(rows):
        target[:, rows] = source[rows, :].astype(F32).T.astype(BF)

    row_loop(LANES, step, source.shape[0])


def cotangent_body(counts, cotangent, gd, gd_t, wide):
    def write(rows, values, slot):
        live = jnp.where(counts[0, slot[4]] > slot[5], 1.0, 0.0)
        values = values * live
        gd[rows, :] = values.astype(BF)
        gd_t[:, rows] = values.T.astype(BF)

    spread(cotangent, wide, write)


class Order:
    def __init__(self, shards, bits):
        self.shards, self.bits = shards, bits

    def shard(self, place):
        count = len(self.bits)
        return sum(bit for n, bit in enumerate(self.bits) if (place >> (count - 1 - n)) & 1)


def store_ordered(scratch, me, order, col, width, send, keep):
    size = scratch.shape[0] // order.shards
    half = order.shards // 2
    for place in range(order.shards):
        source = pl.ds(pl.multiple_of((me ^ order.shard(place)) * size, size), size)
        target, base = (keep, place) if place < half else (send, place - half)
        target[base * size : (base + 1) * size, :] = scratch[source, col : col + width]


def emit(left_t, right, scratch, me, plan, refs, base=0, size=None):
    size = size or right.shape[1]
    step = 256 if size % 256 == 0 else LANES
    for col in range(0, size, step):
        scratch[:, col : col + step] = nn(left_t[...], right[:, base + col : base + col + step])
    hand_out(scratch, me, plan, refs)


def hand_out(scratch, me, plan, refs):
    col = 0
    for n, (order, width) in enumerate(plan):
        if order is None:
            refs[n][...] = scratch[:, col : col + width]
        else:
            store_ordered(scratch, me, order, col, width, refs[2 * n], refs[2 * n + 1])
        col += width


def emitted(dim, plan):
    outs = []
    for order, width in plan:
        if order is None:
            outs.append(((dim, width), F32))
        else:
            outs += [((dim // 2, width), F32)] * 2
    return outs


def product_body(transposed, left, right, out):
    out[...] = (nt if transposed else nn)(left[...], right[...])


def mid_back_body(gain, own, got, middle, gd, out_weight, grad_middle, attended_t, gm, sums, attended):
    total = jnp.zeros(sums.shape, F32)
    for i in range(PADDED // LANES):
        rows = slice(i * LANES, (i + 1) * LANES)
        grad_out = gd[rows, :].astype(F32)
        grad = part_of(own, i) + part_of(got, i)
        back, gain_sum, shift_sum = norm_back(part_of(middle, i), row(gain), grad)
        whole = grad_out + back
        grad_middle[rows, :] = whole
        grad_middle.send(i)
        short = whole.astype(BF)
        wide = short.astype(F32)
        attended[rows, :] = short
        attended_t[:, rows] = wide.T.astype(BF)
        parts = [gain_sum, shift_sum, jnp.sum(wide, axis=0, keepdims=True), jnp.sum(grad_out, axis=0, keepdims=True)]
        total += jnp.concatenate(parts + [jnp.zeros((4, wide.shape[1]), F32)])
    sums[...] = total
    gm[...] = nt(attended[...], out_weight[...]).astype(BF)


def attend_back_body(plan, qkv, mixed_a, mixed_b, lse_a, lse_b, gm, grads, sums, stats_t, delta_t):
    width = qkv.shape[1] // 3
    heads = width // HEAD_DIM
    scale = HEAD_DIM ** (-0.5)
    for start, length, room, part, offset in plan:
        mixed, lse = ((mixed_a, lse_a), (mixed_b, lse_b))[part]
        for i in range(room // LANES):
            at = slice(start + i * LANES, start + (i + 1) * LANES)
            loc = slice(offset + i * LANES, offset + (i + 1) * LANES)
            stats_t[:, at] = lse[loc, :].T
            lane = lax.broadcasted_iota(jnp.int32, (LANES, LANES), 1)
            delta = jnp.zeros((LANES, LANES), F32)
            for head in range(heads):
                pair = slice(head // 2 * PAIR, (head // 2 + 1) * PAIR)
                prod = gm[at, pair].astype(F32) * mixed[loc, pair].astype(F32)
                one = jnp.sum(jnp.where(head_mask(LANES, head % 2), prod, 0.0), axis=-1, keepdims=True)
                delta = jnp.where(lane == head, one, delta)
            delta_t[:, at] = delta.T
        tall = up_to(length, 16)
        valid = lax.broadcasted_iota(jnp.int32, (tall, room), 0) < length
        for pair in range(heads // 2):
            cols = slice(pair * PAIR, (pair + 1) * PAIR)
            q = qkv[start : start + room, cols]
            k = qkv[start : start + tall, width + pair * PAIR : width + (pair + 1) * PAIR]
            v = qkv[start : start + tall, 2 * width + pair * PAIR : 2 * width + (pair + 1) * PAIR]
            do = gm[start : start + room, cols]
            k_t = k.astype(F32).T.astype(BF)
            scores = nt(both_heads(k), q)
            grad_probs = nt(both_heads(v), do)
            probs, grad_scores, grad_q = [], [], []
            for which in range(2):
                head = 2 * pair + which
                at = slice(which * tall, (which + 1) * tall)
                prob = jnp.exp(scores[at] - stats_t[head : head + 1, start : start + room])
                if tall != length:
                    prob = jnp.where(valid, prob, 0.0)
                grad = (prob * (grad_probs[at] - delta_t[head : head + 1, start : start + room])).astype(BF)
                probs.append(prob.astype(BF))
                grad_scores.append(grad)
                grad_q.append(nn(k_t[which * HEAD_DIM : (which + 1) * HEAD_DIM, :], grad))
            grad_v = join_heads(nn(jnp.concatenate(probs), do))
            grad_k = join_heads(nn(jnp.concatenate(grad_scores), q))
            turned = jnp.concatenate(grad_q, axis=0).T
            grads[start : start + room, cols] = (turned.astype(BF).astype(F32) * scale).astype(BF)
            for base, value in ((width, grad_k), (2 * width, grad_v)):
                at = slice(base + pair * PAIR, base + (pair + 1) * PAIR)
                grads[start : start + tall, at] = value.astype(BF)
                if tall != room:
                    grads[start + tall : start + room, at] = jnp.zeros((room - tall, PAIR), BF)
    sums[...] = jnp.zeros_like(sums)

    def step(rows):
        sums[0:1, :] += jnp.sum(grads[rows, :].astype(F32), axis=0, keepdims=True)

    row_loop(LANES, step)


def normed_back_body(grads, weights, out):
    width = weights.shape[2]
    out[...] = sum(nt(grads[:, n * width : (n + 1) * width], weights[n]) for n in range(3))


def project_back_body(plan, base, size, me, left_t, right, *refs):
    emit(left_t, right, refs[-1], me[0], plan, refs[:-1], base, size)


def out_and_project_back_body(plan, me, attended_t, mixed_a, mixed_b, normed_t, grads, *refs):
    mixed, scratch = refs[-2:]
    mixed[:SPLIT, :] = mixed_a[...]
    mixed[SPLIT:, :] = mixed_b[...]
    width = mixed.shape[1]
    scratch[:, :width] = nn(attended_t[...], mixed[...])
    scratch[:, width:] = nn(normed_t[...], grads[:, :width])
    hand_out(scratch, me[0], plan, refs[:-2])


def input_back_body(gain, tok, own, got, grad_middle, sums_two, sums_qkv, gh_sum, grad, small, wide):
    totals = [jnp.zeros((1, grad.shape[1]), F32)] * 2

    def read(rows, slot):
        i = rows.start // LANES
        back, *sums = norm_back(part_of(tok, i).astype(F32), row(gain), part_of(own, i) + part_of(got, i))
        totals[:] = [total + item for total, item in zip(totals, sums)]
        return part_of(grad_middle, i) + back

    gather(read, wide, grad)
    width = sums_qkv.shape[1] // 3
    qv = jnp.concatenate([sums_qkv[0:1, :width], sums_qkv[0:1, 2 * width :]], axis=1)
    two = [sums_two[n : n + 1, :] for n in (2, 0, 1, 3)]
    small[...] = jnp.zeros_like(small)
    for n, item in enumerate([*totals, *two, qv, gh_sum[:, : grad.shape[1]], gh_sum[:, grad.shape[1] :]]):
        small[n : n + 1, :] = item


def output_body(counts, add, middle, own, got, out, wide):
    def read(rows, slot):
        i = rows.start // LANES
        live = jnp.where(counts[0, slot[4]] > slot[5], 1.0, 0.0)
        return live * (part_of(middle, i) + (part_of(own, i) + part_of(got, i) + row(add)))

    gather(read, wide, out)


def swap(value):
    return lax.ppermute(value, "tensor", [(0, 1), (1, 0)])


def exchange(value, bit, shards):
    return lax.ppermute(value, "dp", [(i, i ^ bit) for i in range(shards)])


ORDERS = {
    "A": (1, 2, 4, 8),
    "B": (2, 1, 4, 8),
    "C": (4, 8, 1, 2),
    "D": (4, 8, 2, 1),
    "E": (1, 4, 8, 2),
    "F": (2, 4, 8, 1),
    "G": (4, 1, 2, 8),
    "H": (4, 2, 1, 8),
    "I": (1, 4, 2, 8),
    "J": (2, 4, 1, 8),
    "K": (4, 1, 8, 2),
    "L": (4, 2, 8, 1),
}
PIECES = {
    "GDA": [("da", 768, "A")],
    "GDB": [("db", 768, "G")],
    "GUA": [("ua", 768, "J")],
    "GUB": [("ub", 768, "A")],
    "QA": [("qa", 768, "B")],
    "QB": [("qb", 768, "H")],
}
TURNS = ["A0", "A1", "CT", "T1", "H", "UB", "T2", "GDA", "GUA", "GDB", "MB", "AB"]
TURNS += ["NB", "da+0", "ua+0", "db+0", "QA", "GUB", "da+1", "db+1", "QB", "ua+1", "da+2", "qa+0"]
TURNS += ["ub+0", "IB", "ua+2", "qb+0", "db+2", "ub+1", "ua+3", "da+3", "s+0", "qb+1", "db+3", "ub+2"]
TURNS += ["qa+1", "DN", "s+1", "qb+2", "OUT", "qa+2", "ub+3", "s+2", "qa+3", "s+3", "qb+3"]


def per_device(
    shards,
    tokens,
    counts,
    cotangent,
    ln1_gain,
    ln1_bias,
    qkv_weight,
    qv_bias,
    out_weight,
    out_bias,
    ln2_gain,
    ln2_bias,
    up_weight,
    up_bias,
    down_weight,
    down_bias,
):
    dim = tokens.shape[1]
    width = qkv_weight.shape[2]
    units = up_weight.shape[1]
    weights = jnp.transpose(qkv_weight, (1, 0, 2))
    me = lax.axis_index("dp").astype(jnp.int32)
    place = me.reshape(1)
    ordered = shards == 16
    have, pieces, last = {}, {}, [None]

    def plan_of(kernel):
        return [(Order(shards, ORDERS[order]) if ordered else None, cols) for _, cols, order in PIECES[kernel]]

    def tied(value):
        if last[0] is None:
            return value
        return lax.optimization_barrier((value, last[0]))[0]

    def ran(outs):
        last[0] = outs[0]
        return outs

    def leave(kernel, outs):
        ran(outs)
        for n, (name, _, order) in enumerate(PIECES[kernel]):
            if ordered:
                send, keep = outs[2 * n : 2 * n + 2]
                bits = ORDERS[order]
                pieces[name] = (exchange(send, bits[0], shards), keep, bits)
            else:
                pieces[name] = outs[n]

    parts = PADDED // LANES

    def attend_plan(kind):
        plan = [(dst, length, room, dst - kind * SPLIT) for _, length, dst, room, k, _ in SLOTS if k == kind]
        count = sum(p[2] for p in plan)
        return plan, [((count, width), BF, 1), ((count, LANES), F32, 1), ((count, dim), F32)]

    def kernel_a0():
        plan, results = attend_plan(0)
        fetched = [cotangent, up_weight, down_weight]
        outs = call(
            functools.partial(front_body, plan),
            [((PADDED, dim), BF), ((PADDED, dim), BF), ((PADDED, dim), BF, 0), ((PADDED, 3 * width), BF, 1)]
            + results
            + [((PADDED - SPLIT, 3 * width), BF), ((width, dim), BF)]
            + [(item.shape, BF) for item in fetched],
            [place]
            + [Far(item) for item in (tokens, ln1_gain, ln1_bias, weights, qv_bias)]
            + [Far(out_weight, wait=True)]
            + [Far(item, chunks=0) for item in fetched],
            scratch=[((WIDE, dim), F32)],
            smem=1,
            sems=len(fetched) + 1,
            name="front",
            room=12,
        )
        have["near"], have["normed"], have["tok"], have["qkv"] = outs[:4]
        have["mixed", 0], have["lse", 0], have["part", 0], have["rest"], have["out_weight"] = outs[4:9]
        have["cotangent"], have["up"], have["down"] = outs[9:]
        ran(outs)
        have["got", 0] = swap(have["part", 0])

    def kernel_a1():
        plan, results = attend_plan(1)
        outs = call(
            functools.partial(attend_body, [(local, length, room, local) for _, length, room, local in plan]),
            results,
            [tied(have["rest"]), have["out_weight"]],
            name="attend",
            room=4,
        )
        have["mixed", 1], have["lse", 1], have["part", 1] = ran(outs)
        have["got", 1] = swap(outs[2])

    def kernel_ct():
        outs = call(
            cotangent_body,
            [((PADDED, dim), BF), ((dim, PADDED), BF)],
            [counts, tied(have["cotangent"])],
            scratch=[((WIDE, dim), F32)],
            smem=1,
            name="cotangent",
        )
        have["gd"], have["gd_t"] = ran(outs)

    def kernel_h():
        near = [have[what, kind] for kind in range(2) for what in ("part", "got")]
        outs = call(
            hidden_body,
            [((PADDED, dim), F32), ((PADDED, dim), BF), ((PADDED, units), BF), ((PADDED, units), BF), ((1, units), F32)],
            [tied(have["near"]), Far(out_bias), Far(ln2_gain), Far(ln2_bias), *near]
            + [have["up"], Far(up_bias), have["gd"], have["down"]],
            name="hidden",
            room=8,
        )
        have["middle"], have["normed_two"], have["act"], have["gh"], have["gh_sum"] = outs
        ran(outs[1:])

    def kernel_g(kernel, left_t, right, base):
        plan = plan_of(kernel)
        size = units // 2
        outs = call(
            functools.partial(project_back_body, plan, base, size),
            emitted(dim, plan),
            [place, tied(have[left_t]), have[right]],
            scratch=[((dim, size), F32)],
            smem=1,
            name="mlp_" + kernel.lower(),
            room=3,
        )
        leave(kernel, ran(outs))

    def kernel_sum(transposed, source, weight, target, name):
        outs = call(
            functools.partial(product_body, transposed),
            [((PADDED, dim), F32)],
            [tied(have[source]), weight],
            name=name,
            room=8,
        )
        (have["part", target],) = ran(outs)
        have["got", target] = swap(outs[0])

    def kernel_t(source, target):
        (have[target],) = ran(
            call(transpose_body, [((dim, PADDED), BF)], [tied(have[source])], name="turn_" + source)
        )

    def kernel_mb():
        outs = call(
            mid_back_body,
            [((PADDED, dim), F32, parts), ((dim, PADDED), BF), ((PADDED, width), BF), ((8, dim), F32)],
            [Far(ln2_gain), tied(have["part", "gn"]), have["got", "gn"], have["middle"], have["gd"], have["out_weight"]],
            scratch=[((PADDED, dim), BF)],
            name="middle_back",
            room=12,
        )
        have["grad_middle"], have["attended_t"], have["gm"], have["sums_two"] = outs
        ran(outs[1:])

    def kernel_ab():
        plan = []
        for _, length, dst, room, kind, _ in SLOTS:
            plan.append((dst, length, room, kind, dst - kind * SPLIT))
        outs = call(
            functools.partial(attend_back_body, plan),
            [((PADDED, 3 * width), BF), ((8, 3 * width), F32)],
            [Far(tied(have["qkv"]))]
            + [Far(have[what, kind]) for what in ("mixed", "lse") for kind in range(2)]
            + [have["gm"]],
            scratch=[((LANES, PADDED), F32), ((LANES, PADDED), F32)],
            name="attend_back",
            room=8,
        )
        have["grads"], have["sums_qkv"] = ran(outs)

    def kernel_qa():
        plan = plan_of("QA")
        leave(
            "QA",
            call(
                functools.partial(out_and_project_back_body, plan),
                emitted(dim, plan),
                [place, tied(have["attended_t"]), Far(have["mixed", 0]), Far(have["mixed", 1]), have["normed_t"]]
                + [have["grads"]],
                scratch=[((PADDED, width), BF), ((dim, 2 * width), F32)],
                smem=1,
                name="project_back_a",
                room=3,
            ),
        )

    def kernel_qb():
        plan = plan_of("QB")
        leave(
            "QB",
            call(
                functools.partial(project_back_body, plan, width, 2 * width),
                emitted(dim, plan),
                [place, tied(have["normed_t"]), have["grads"]],
                scratch=[((dim, 2 * width), F32)],
                smem=1,
                name="project_back_b",
                room=3,
            ),
        )

    def kernel_nb():
        outs = call(
            normed_back_body, [((PADDED, dim), F32)], [tied(have["grads"]), Far(weights)], name="normed_back", room=6
        )
        (have["part", "n"],) = ran(outs)
        have["got", "n"] = swap(outs[0])

    def kernel_out():
        outs = call(
            output_body,
            [((ROWS, dim), BF)],
            [counts, Far(down_bias), tied(have["middle"]), have["part", "out"], have["got", "out"]],
            scratch=[((WIDE, dim), F32)],
            smem=1,
            name="output",
            room=8,
        )
        (have["output"],) = ran(outs)

    def kernel_ib():
        outs = call(
            input_back_body,
            [((ROWS, dim), BF), ((16, dim), F32)],
            [Far(ln1_gain), Far(have["tok"], parts), tied(have["part", "n"]), have["got", "n"]]
            + [Far(have["grad_middle"], parts), have["sums_two"], have["sums_qkv"]]
            + [have["gh_sum"]],
            scratch=[((WIDE, dim), F32)],
            name="input_back",
            room=6,
        )
        have["input_grad"], small = ran(outs)
        pieces["s"] = (exchange(small, 1, shards), small) if ordered else lax.psum(small, "dp")

    kernels = {
        "A0": kernel_a0,
        "A1": kernel_a1,
        "CT": kernel_ct,
        "T1": lambda: kernel_t("normed", "normed_t"),
        "T2": lambda: kernel_t("normed_two", "normed_two_t"),
        "H": kernel_h,
        "GDA": lambda: kernel_g("GDA", "gd_t", "act", 0),
        "GDB": lambda: kernel_g("GDB", "gd_t", "act", units // 2),
        "GUA": lambda: kernel_g("GUA", "normed_two_t", "gh", 0),
        "GUB": lambda: kernel_g("GUB", "normed_two_t", "gh", units // 2),
        "UB": lambda: kernel_sum(True, "gh", have["up"], "gn", "up_back"),
        "DN": lambda: kernel_sum(False, "act", Far(down_weight), "out", "down"),
        "MB": kernel_mb,
        "AB": kernel_ab,
        "QA": kernel_qa,
        "QB": kernel_qb,
        "NB": kernel_nb,
        "OUT": kernel_out,
        "IB": kernel_ib,
    }

    def add(name, step):
        if name == "s":
            got, own = pieces[name]
            total = tied(got) + own
            last[0] = total
            pieces[name] = (exchange(total, 2 << step, shards), total) if step < 3 else total
            return
        got, keep, bits = pieces[name]
        got = tied(got)
        if step == 3:
            pieces[name] = last[0] = got + keep
            return
        half = got.shape[0] // 2
        send, keep = got[half:] + keep[half:], got[:half] + keep[:half]
        last[0] = send
        pieces[name] = (exchange(send, bits[step + 1], shards), keep, bits)

    for turn in TURNS:
        if turn in kernels:
            kernels[turn]()
        elif ordered:
            name, step = turn.split("+")
            add(name, int(step))

    def gathered(kernel):
        return [pieces[name] for name, _, _ in PIECES[kernel]]

    down_grad = jnp.concatenate(gathered("GDA") + gathered("GDB"), axis=1)
    up_grad = jnp.concatenate(gathered("GUA") + gathered("GUB"), axis=1)
    (first,), (second,) = gathered("QA"), gathered("QB")
    if not ordered:
        first, second, up_grad, down_grad = (
            lax.psum_scatter(item, "dp", scatter_dimension=0, tiled=True) for item in (first, second, up_grad, down_grad)
        )
    out_grad = first[:, :width]
    qkv_grad = jnp.concatenate([first[:, width:], second], axis=1)
    small = pieces["s"]
    mine = lax.dynamic_slice_in_dim(small[:6], me * (dim // shards), dim // shards, 1)
    rest = small[6:9].reshape(-1)
    return (
        have["output"],
        have["input_grad"],
        mine[0],
        mine[1],
        qkv_grad.reshape(dim // shards, 3, width),
        rest[: 2 * width].reshape(2, width),
        out_grad.T,
        mine[2],
        mine[3],
        mine[4],
        up_grad,
        rest[2 * width :],
        down_grad.T,
        mine[5],
    )


def solution(mesh):
    in_specs = (
        P("dp", None),
        P("dp", None),
        P("dp", None),
        P(),
        P(),
        P(None, None, "tensor"),
        P(None, "tensor"),
        P("tensor", None),
        P(),
        P(),
        P(),
        P(None, "tensor"),
        P("tensor"),
        P("tensor", None),
        P(),
    )
    out_specs = (
        P("dp", None),
        P("dp", None),
        P("dp"),
        P("dp"),
        P("dp", None, "tensor"),
        P(None, "tensor"),
        P("tensor", "dp"),
        P("dp"),
        P("dp"),
        P("dp"),
        P("dp", "tensor"),
        P("tensor"),
        P("tensor", "dp"),
        P("dp"),
    )
    return jax.shard_map(
        functools.partial(per_device, mesh.shape["dp"]),
        mesh=mesh,
        in_specs=in_specs,
        out_specs=out_specs,
        check_vma=False,
    )
```

```python
import enum
import functools
import math
import types

import jax
import jax.numpy as jnp
from jax import lax
from jax.experimental import pallas as pl
from jax.experimental.pallas import tpu as pltpu
from jax.sharding import PartitionSpec as P

HEAD_DIM = 64
LONG_LEN = 608
SHORT_LEN = 228
LONG_SLOTS = 1
SHORT_SLOTS = 2
EPS = 1e-06

DP, TENSOR = "dp", "tensor"
LANES = 128
PAIR = 2 * HEAD_DIM
BF = jnp.bfloat16
F32 = jnp.float32
VMEM_LIMIT = 60 * 1024 * 1024


def up_to(value, unit):
    return -(-value // unit) * unit


def slots():
    found, src, dst = [], 0, 0
    for kind, (number, length) in enumerate(((LONG_SLOTS, LONG_LEN), (SHORT_SLOTS, SHORT_LEN))):
        for index in range(number):
            room = up_to(length, LANES)
            found.append((src, length, dst, room, kind, index))
            src, dst = src + length, dst + room
    return found, src, dst


SLOTS, ROWS, PADDED = slots()
SPLIT = sum(slot[3] for slot in SLOTS if slot[4] == 0)
CHUNK = PADDED // 3


def row(ref):
    return ref[...].reshape(1, -1)


def nn(left, right):
    return lax.dot_general(left, right, (((1,), (0,)), ((), ())), preferred_element_type=F32)


def nt(left, right):
    return lax.dot_general(left, right, (((1,), (1,)), ((), ())), preferred_element_type=F32)


NAMES = ("A0", "A1", "CT", "T1", "H", "H2", "T2", "GA", "GB", "UB", "DN", "MB", "AB", "QA", "QB", "NB", "IB", "OUT")
Kernel = enum.Enum("Kernel", NAMES)
Piece = enum.Enum("Piece", ("GA", "GB", "QA", "QB", "S"))
K, P_ = Kernel, Piece
TURNS = [
    K.A0, K.A1, K.CT, K.T1, K.H, K.GA, K.H2, K.T2, K.GB, K.UB, K.MB, (P_.GA, 0), K.AB, K.NB, (P_.GA, 1), K.QA,
    (P_.GB, 0), (P_.GA, 2), K.QB, K.IB, K.DN, (P_.GB, 1), (P_.S, 0), (P_.QA, 0), (P_.QB, 0), (P_.GB, 2), (P_.QB, 1),
    (P_.GA, 3), (P_.QA, 1), (P_.QB, 2), (P_.GB, 3), (P_.QA, 2), K.OUT, (P_.QB, 3), (P_.QA, 3),
]
PIECES = {
    K.GA: (P_.GA, 1536, ((2, 1, 4, 8), (4, 8, 2, 1))),
    K.GB: (P_.GB, 1536, ((2, 4, 1, 8), (1, 2, 4, 8))),
    K.QA: (P_.QA, 768, ((1, 4, 2, 8), (1, 2, 4, 8))),
    K.QB: (P_.QB, 768, ((4, 2, 1, 8), (2, 1, 4, 8))),
}
COSTS = {
    K.A1: 1000000000,
    K.UB: 10000000000,
    K.AB: 10000000000,
    K.A0: 3000000000,
    K.OUT: 1000000000,
    K.H: 1000000000,
    K.CT: 1000000000,
    K.T2: 1000000000,
    K.IB: 3000000000,
    K.T1: 1000000000,
    K.NB: 1000000000,
    K.QA: 10000000000,
    K.H2: 1000000000,
    K.GA: 1000000000,
    K.GB: 3000000000,
    K.MB: 1000000000,
    K.DN: 1000000000,
    K.QB: 3000000000,
}


def held(shape, dtype):
    shape = (1, *shape)
    lead = math.prod(shape[:-2])
    return lead * up_to(shape[-2], 16) * up_to(shape[-1], LANES) * jnp.dtype(dtype).itemsize


class Far:
    def __init__(self, value, chunks=1, rows=None, cols=None, wait=False):
        self.value, self.chunks, self.rows, self.cols, self.wait = value, chunks, rows, cols, wait

    @property
    def shape(self):
        shape = list(self.value.shape)
        if self.rows is not None:
            shape[0] = self.rows[1]
        if self.cols is not None:
            shape[-1] = self.cols[1]
        return tuple(shape)

    @property
    def dtype(self):
        return self.value.dtype


class Late:
    def __init__(self, spec, source, buffer, sems):
        self.buffer, self.left = buffer, {}
        if spec.rows is not None:
            source = source.at[pl.ds(*spec.rows)]
        if spec.cols is not None:
            source = source.at[..., pl.ds(*spec.cols)]
        size = spec.shape[0] // spec.chunks
        for i in range(spec.chunks):
            parts = (source, buffer)
            if spec.chunks > 1:
                parts = (ref.at[i * size : (i + 1) * size] for ref in parts)
            self.left[i] = pltpu.make_async_copy(*parts, sems.at[i])
        if not spec.wait:
            self.start()

    def start(self):
        for copy in self.left.values():
            copy.start()

    def rows(self, i):
        if i in self.left:
            self.left.pop(i).wait()
        return self.buffer

    def all(self):
        for i in list(self.left):
            self.rows(i)
        return self.buffer

    @property
    def shape(self):
        return self.buffer.shape

    def __getitem__(self, key):
        return self.all()[key]


def part_of(ref, i):
    rows = slice(i * LANES, (i + 1) * LANES)
    return ref.rows(i)[rows, :] if isinstance(ref, Late) else ref[rows, :]


class Away:
    def __init__(self, buffer, target, sems, chunks):
        self.buffer, self.target, self.sems, self.chunks, self.sent = buffer, target, sems, chunks, []

    @property
    def shape(self):
        return self.buffer.shape

    def __setitem__(self, key, value):
        self.buffer[key] = value

    def __getitem__(self, key):
        return self.buffer[key]

    def send(self, i=None):
        parts = (self.buffer, self.target)
        if i is not None:
            size = self.buffer.shape[0] // self.chunks
            parts = (ref.at[i * size : (i + 1) * size] for ref in parts)
        copy = pltpu.make_async_copy(*parts, self.sems.at[i or 0])
        copy.start()
        self.sent.append(copy)


def call(kernel, body, outs, args, scratch=(), smem=0, sems=0, room=4):
    specs = [pl.BlockSpec(memory_space=pltpu.SMEM)] * smem
    buffers = []
    for arg in args[smem:]:
        far = isinstance(arg, Far)
        specs.append(pl.BlockSpec(memory_space=pl.ANY if far else pltpu.VMEM))
        if far:
            if arg.chunks:
                buffers += [pltpu.VMEM(arg.shape, arg.dtype), pltpu.SemaphoreType.DMA((arg.chunks,))]
    for out in outs:
        if len(out) > 2 and out[2]:
            buffers += [pltpu.VMEM(out[0], out[1]), pltpu.SemaphoreType.DMA((out[2],))]
    need = sum(held(*item[:2]) for item in [*(out for out in outs if len(out) > 2 and out[2]), *scratch])
    need += sum(held(arg.shape, arg.dtype) for arg in args[smem:] if isinstance(arg, Far) and arg.chunks)
    spaces = [pltpu.SMEM] * smem + [pltpu.HBM if isinstance(arg, Far) else pltpu.VMEM for arg in args[smem:]]
    values = [arg.value if isinstance(arg, Far) else arg for arg in args]
    values[smem:] = [pltpu.with_memory_space_constraint(*pair) for pair in zip(values[smem:], spaces[smem:])]

    def run(*refs):
        given, refs = refs[: len(args)], refs[len(args) :]
        made, refs = refs[: len(outs)], refs[len(outs) :]
        count = len(scratch) + (1 if sems else 0)
        own, extra = refs[:count], list(refs[count:])
        ins, results = [], []
        for arg, ref in zip(args, given):
            late = isinstance(arg, Far) and arg.chunks
            ins.append(Late(arg, ref, extra.pop(0), extra.pop(0)) if late else ref)
        for out, ref in zip(outs, made):
            away = len(out) > 2 and out[2]
            results.append(Away(extra.pop(0), ref, extra.pop(0), out[2]) if away else ref)
        body(*ins, *results, *own)
        for item in ins:
            if isinstance(item, Late):
                item.all()
        for item in results:
            if isinstance(item, Away):
                for copy in item.sent:
                    copy.wait()

    return pl.pallas_call(
        run,
        out_shape=[pltpu.HBM(*out[:2]) if len(out) > 2 else pltpu.VMEM(*out) for out in outs],
        in_specs=specs,
        out_specs=[pl.BlockSpec(memory_space=pl.ANY if len(out) > 2 else pltpu.VMEM) for out in outs],
        scratch_shapes=[pltpu.VMEM(*item) for item in scratch]
        + ([pltpu.SemaphoreType.DMA((sems,))] if sems else [])
        + buffers,
        compiler_params=pltpu.CompilerParams(vmem_limit_bytes=need + room * 2**20),
        cost_estimate=pl.CostEstimate(flops=COSTS.get(kernel, 1000), bytes_accessed=1000, transcendentals=0),
        name=kernel.name.lower(),
    )(*values)


def row_loop(step, body, rows=PADDED):
    def run(i, carry):
        body(pl.ds(pl.multiple_of(i * step, step), step))
        return carry

    lax.fori_loop(0, rows // step, run, 0)


def normal_parts(values):
    center = values - jnp.mean(values, axis=-1, keepdims=True)
    spread = jnp.mean(center * center, axis=-1, keepdims=True)
    ratio = lax.rsqrt(spread + EPS)
    return center * ratio, ratio


def norm_back(values, gain, grad):
    hat, ratio = normal_parts(values)
    scaled = grad * gain
    mean_one = jnp.mean(scaled, axis=-1, keepdims=True)
    mean_two = jnp.mean(scaled * hat, axis=-1, keepdims=True)
    back = ratio * (scaled - mean_one - hat * mean_two)
    return back, jnp.sum(grad * hat, axis=0, keepdims=True), jnp.sum(grad, axis=0, keepdims=True)


def spread(source, wide, write):
    wide[:ROWS, :] = source[...].astype(F32)
    for slot in SLOTS:
        src, length, dst, room = slot[:4]
        for i in range(0, room, LANES):
            values = wide[src + i : src + i + LANES, :]
            if i + LANES > length:
                row = lax.broadcasted_iota(jnp.int32, values.shape, 0)
                values = jnp.where(row < length - i, values, 0.0)
            write(slice(dst + i, dst + i + LANES), values, slot)


def gather(read, wide, target):
    for slot in SLOTS:
        src, _, dst, room = slot[:4]
        for i in range(0, room, LANES):
            wide[src + i : src + i + LANES, :] = read(slice(dst + i, dst + i + LANES), slot)
    target[...] = wide[:ROWS, :].astype(BF)


WIDE = up_to(ROWS + LANES, LANES)


def project_body(tokens, gain, shift, weight, bias, tok, normed, qkv, wide, copies):
    width = weight.shape[1] // 3
    scale = HEAD_DIM ** (-0.5)

    def write(rows, values, slot):
        tok[rows, :] = values.astype(BF)
        hat, _ = normal_parts(values)
        normed[rows, :] = (hat * row(gain) + row(shift)).astype(BF)

    spread(tokens, wide, write)
    for copy in copies:
        copy.wait()
    for start in range(0, PADDED, CHUNK):
        rows = slice(start, start + CHUNK)
        proj = nn(normed[rows, :], weight[...])
        qkv[rows, :width] = ((proj[:, :width] + bias[0:1, :]) * scale).astype(BF)
        qkv[rows, width : 2 * width] = proj[:, width : 2 * width].astype(BF)
        qkv[rows, 2 * width :] = (proj[:, 2 * width :] + bias[1:2, :]).astype(BF)
    qkv.send()


UNIT = 256


def head_mask(rows, which):
    lane = lax.broadcasted_iota(jnp.int32, (rows, PAIR), 1)
    return (lane // HEAD_DIM) == which


def both_heads(block):
    zero = jnp.zeros_like(block)
    return jnp.concatenate([jnp.where(head_mask(block.shape[0], which), block, zero) for which in range(2)])


def join_heads(block):
    half = block.shape[0] // 2
    return jnp.where(head_mask(half, 0), block[:half], block[half:])


def attend_body(plan, qkv, out_weight, mixed, lse, part):
    width = qkv.shape[1] // 3
    for start, length, room, local in plan:
        lane = lax.broadcasted_iota(jnp.int32, (room, LANES), 1)
        keep = lax.broadcasted_iota(jnp.int32, (1, room), 1) < length
        stats = jnp.zeros((room, LANES), F32)

        def scores_of(pair):
            q, k = (qkv[start : start + room, at : at + PAIR] for at in (pair * PAIR, width + pair * PAIR))
            return jnp.where(keep, nt(both_heads(q), k), -1e30)

        scores = scores_of(0)
        for pair in range(width // PAIR):
            later = scores_of(pair + 1) if pair + 1 < width // PAIR else None
            v = qkv[start : start + room, 2 * width + pair * PAIR : 2 * width + (pair + 1) * PAIR]
            top = jnp.max(scores, axis=-1, keepdims=True)
            expo = jnp.exp(scores - top)
            total = jnp.sum(expo, axis=-1, keepdims=True)
            out = nn(expo.astype(BF), v) / total
            mixed[local : local + room, pair * PAIR : (pair + 1) * PAIR] = join_heads(out).astype(BF)
            log_total = top + jnp.log(total)
            stats = jnp.where(lane == 2 * pair, log_total[:room], stats)
            stats = jnp.where(lane == 2 * pair + 1, log_total[room:], stats)
            scores = later
        lse[local : local + room, :] = stats
    mixed.send()
    lse.send()
    part[...] = nn(mixed[...], out_weight[...])


def front_body(plan, me, tokens, gain, shift, weight, bias, out_weight, *refs):
    fetched, (tok, normed, tok_far), (qkv, mixed, lse, part, rest, kept) = refs[:3], refs[3:6], refs[6:12]
    targets, (wide, flat, sems) = refs[12:15], refs[15:]
    width = flat.shape[1] // 3
    first = []
    for n in range(3):
        first.append(pltpu.make_async_copy(weight.at[n], flat.at[:, n * width : (n + 1) * width], sems.at[n]))
        first[n].start()
    copies = [pltpu.make_async_copy(*pair, sems.at[3 + n]) for n, pair in enumerate(zip(fetched, targets))]
    copies.append(pltpu.make_async_copy(tok, tok_far, sems.at[6]))
    project_body(tokens, gain, shift, flat, bias, tok, normed, qkv, wide, first)
    out_weight.start()
    for copy in copies:
        copy.start()
    rest[...] = qkv[SPLIT:, :]
    attend_body(plan, qkv, out_weight, mixed, lse, part)
    kept[...] = out_weight[...]
    for copy in copies:
        copy.wait()


def hidden_body(tok, add, gain, shift, own_a, got_a, own_b, got_b, up, up_add, middle, normed, act, slope):
    for i in range(PADDED // LANES):
        rows = slice(i * LANES, (i + 1) * LANES)
        base, own, got = (0, own_a, got_a) if i < SPLIT // LANES else (SPLIT, own_b, got_b)
        n = i - base // LANES
        mid = part_of(tok, i).astype(F32) + (part_of(own, n) + part_of(got, n) + row(add))
        middle[rows, :] = mid
        hat, _ = normal_parts(mid)
        normed[rows, :] = (hat * row(gain) + row(shift)).astype(BF)
    for start in range(0, PADDED, CHUNK):
        rows = slice(start, start + CHUNK)
        for col in range(0, act.shape[1], UNIT):
            cols = slice(col, col + UNIT)
            hidden = nn(normed[rows, :], up[:, cols]) + row(up_add)[:, cols]
            cdf = 0.5 + 0.5 * lax.erf(hidden * (2.0**-0.5))
            act[rows, cols] = (hidden * cdf).astype(BF)
            slope[rows, cols] = cdf + hidden * (jnp.exp(hidden * hidden * -0.5) * ((2.0 * math.pi) ** -0.5))


def hidden_back_body(gd, slope, down, gh, gh_sum):
    for start in range(0, PADDED, CHUNK):
        rows = slice(start, start + CHUNK)
        for col in range(0, gh.shape[1], UNIT):
            cols = slice(col, col + UNIT)
            gh[rows, cols] = (nt(gd[rows, :], down[cols, :]) * slope[rows, cols]).astype(BF)
    gh_sum[...] = jnp.sum(gh[...].astype(F32), axis=0, keepdims=True)


def transpose_body(source, target):
    source = source.all() if isinstance(source, Late) else source
    def step(rows):
        target[:, rows] = source[rows, :].astype(F32).T.astype(BF)

    row_loop(LANES, step, source.shape[0])


def cotangent_body(counts, cotangent, gd, gd_t, wide):
    def write(rows, values, slot):
        live = jnp.where(counts[0, slot[4]] > slot[5], 1.0, 0.0)
        values = values * live
        gd[rows, :] = values.astype(BF)
        gd_t[:, rows] = values.T.astype(BF)

    spread(cotangent, wide, write)


class Order:
    def __init__(self, shards, bits):
        self.shards, self.bits = shards, bits

    def shard(self, place, core):
        count = len(self.bits[0])
        found = [sum(bit for n, bit in enumerate(bits) if (place >> (count - 1 - n)) & 1) for bits in self.bits]
        return jnp.where(core == 0, *found)


def store_ordered(scratch, me, order, col, width, send, keep):
    size = scratch.shape[0] // order.shards
    half = order.shards // 2
    for place in range(order.shards):
        source = pl.ds(pl.multiple_of((me[0] ^ order.shard(place, me[1])) * size, size), size)
        target, base = (keep, place) if place < half else (send, place - half)
        target[base * size : (base + 1) * size, :] = scratch[source, col : col + width]


def hand_out(scratch, me, plan, refs):
    col = 0
    for n, (order, width) in enumerate(plan):
        if order is None:
            refs[n][...] = scratch[:, col : col + width]
        else:
            store_ordered(scratch, me, order, col, width, refs[2 * n], refs[2 * n + 1])
        col += width


def emitted(dim, plan):
    outs = []
    for order, width in plan:
        if order is None:
            outs.append(((dim, width), F32))
        else:
            outs += [((dim // 2, width), F32)] * 2
    return outs


def in_chunks(out, product):
    for start in range(0, PADDED, CHUNK):
        rows = slice(start, start + CHUNK)
        out[rows, :] = product(rows)


def up_back_body(left, right, out_a, out_b):
    out_a[...] = nt(left[:SPLIT, :], right[...])
    out_b[...] = nt(left[SPLIT:, :], right[...])


def down_body(left, right, out):
    in_chunks(out, lambda rows: nn(left[rows, :], right[...]))


def mid_back_body(gain, own_a, got_a, own_b, got_b, middle, gd, out_weight, grad_middle, attended_t, gm, sums, attended):
    total = jnp.zeros(sums.shape, F32)
    for i in range(PADDED // LANES):
        rows = slice(i * LANES, (i + 1) * LANES)
        grad_out = gd[rows, :].astype(F32)
        base, own, got = (0, own_a, got_a) if i < SPLIT // LANES else (SPLIT, own_b, got_b)
        grad = part_of(own, i - base // LANES) + part_of(got, i - base // LANES)
        back, gain_sum, shift_sum = norm_back(part_of(middle, i), row(gain), grad)
        whole = grad_out + back
        grad_middle[rows, :] = whole
        grad_middle.send(i)
        short = whole.astype(BF)
        wide = short.astype(F32)
        attended[rows, :] = short
        attended_t[:, rows] = wide.T.astype(BF)
        parts = [gain_sum, shift_sum, jnp.sum(wide, axis=0, keepdims=True), jnp.sum(grad_out, axis=0, keepdims=True)]
        total += jnp.concatenate(parts + [jnp.zeros((4, wide.shape[1]), F32)])
    sums[...] = total
    gm[...] = nt(attended[...], out_weight[...]).astype(BF)


def attend_back_body(plan, qkv, mixed_a, mixed_b, lse_a, lse_b, gm, grads, sums, stats_t, delta_t):
    width = qkv.shape[1] // 3
    heads = width // HEAD_DIM
    scale = HEAD_DIM ** (-0.5)
    for start, length, room, part, offset in plan:
        mixed, lse = ((mixed_a, lse_a), (mixed_b, lse_b))[part]
        for i in range(room // LANES):
            at = slice(start + i * LANES, start + (i + 1) * LANES)
            loc = slice(offset + i * LANES, offset + (i + 1) * LANES)
            stats_t[:, at] = lse[loc, :].T
            lane = lax.broadcasted_iota(jnp.int32, (LANES, LANES), 1)
            delta = jnp.zeros((LANES, LANES), F32)
            for head in range(heads):
                pair = slice(head // 2 * PAIR, (head // 2 + 1) * PAIR)
                prod = gm[at, pair].astype(F32) * mixed[loc, pair].astype(F32)
                one = jnp.sum(jnp.where(head_mask(LANES, head % 2), prod, 0.0), axis=-1, keepdims=True)
                delta = jnp.where(lane == head, one, delta)
            delta_t[:, at] = delta.T
        tall = up_to(length, 16)
        valid = lax.broadcasted_iota(jnp.int32, (tall, room), 0) < length
        for pair in range(heads // 2):
            cols = slice(pair * PAIR, (pair + 1) * PAIR)
            q = qkv[start : start + room, cols]
            k = qkv[start : start + tall, width + pair * PAIR : width + (pair + 1) * PAIR]
            v = qkv[start : start + tall, 2 * width + pair * PAIR : 2 * width + (pair + 1) * PAIR]
            do = gm[start : start + room, cols]
            k_t = k.astype(F32).T.astype(BF)
            scores = nt(both_heads(k), q)
            grad_probs = nt(both_heads(v), do)
            probs, grad_scores, grad_q = [], [], []
            for which in range(2):
                head = 2 * pair + which
                at = slice(which * tall, (which + 1) * tall)
                prob = jnp.exp(scores[at] - stats_t[head : head + 1, start : start + room])
                if tall != length:
                    prob = jnp.where(valid, prob, 0.0)
                grad = (prob * (grad_probs[at] - delta_t[head : head + 1, start : start + room])).astype(BF)
                probs.append(prob.astype(BF))
                grad_scores.append(grad)
                grad_q.append(nn(k_t[which * HEAD_DIM : (which + 1) * HEAD_DIM, :], grad))
            grad_v = join_heads(nn(jnp.concatenate(probs), do))
            grad_k = join_heads(nn(jnp.concatenate(grad_scores), q))
            turned = jnp.concatenate(grad_q, axis=0).T
            grads[start : start + room, cols] = (turned.astype(BF).astype(F32) * scale).astype(BF)
            for base, value in ((width, grad_k), (2 * width, grad_v)):
                at = slice(base + pair * PAIR, base + (pair + 1) * PAIR)
                grads[start : start + tall, at] = value.astype(BF)
                if tall != room:
                    grads[start + tall : start + room, at] = jnp.zeros((room - tall, PAIR), BF)
    sums[0:1, :] = jnp.sum(grads[...].astype(F32), axis=0, keepdims=True)


def normed_back_body(grads, weight, out, flat, sems):
    width = flat.shape[1] // 3
    copies = []
    for n in range(3):
        copies.append(pltpu.make_async_copy(weight.at[n], flat.at[:, n * width : (n + 1) * width], sems.at[n]))
        copies[n].start()
    for copy in copies:
        copy.wait()
    in_chunks(out, lambda rows: nt(grads[rows, :], flat[...]))


def gradient_body(plan, first, me, left_t, right, *refs):
    scratch = refs[-1]
    for col in range(0, scratch.shape[1], 256):
        scratch[:, col : col + 256] = nn(left_t[...], right[:, first + col : first + col + 256])
    hand_out(scratch, me, plan, refs[:-1])


def out_and_query_body(plan, query, me, attended_t, mixed_a, mixed_b, normed_t, grads, *refs):
    mixed, scratch = refs[-2:]
    mixed[:SPLIT, :] = mixed_a[...]
    mixed[SPLIT:, :] = mixed_b[...]
    width = mixed.shape[1]
    scratch[:, :width] = nn(attended_t[...], mixed[...])
    scratch[:, width:] = nn(normed_t[...], grads[:, :query])
    hand_out(scratch, me, plan, refs[:-2])


def input_back_body(gain, tok, own, got, grad_middle, sums_two, sums_qkv, gh_sum, grad, small, wide):
    totals = [jnp.zeros((1, grad.shape[1]), F32)] * 2

    def read(rows, slot):
        i = rows.start // LANES
        back, *sums = norm_back(part_of(tok, i).astype(F32), row(gain), part_of(own, i) + part_of(got, i))
        totals[:] = [total + item for total, item in zip(totals, sums)]
        return part_of(grad_middle, i) + back

    gather(read, wide, grad)
    grad.send()
    width = sums_qkv.shape[1] // 3
    qv = jnp.concatenate([sums_qkv[0:1, :width], sums_qkv[0:1, 2 * width :]], axis=1)
    two = [sums_two[n : n + 1, :] for n in (2, 0, 1, 3)]
    small[...] = jnp.zeros_like(small)
    for n, item in enumerate([*totals, *two, qv, gh_sum[:, : grad.shape[1]], gh_sum[:, grad.shape[1] :]]):
        small[n : n + 1, :] = item


def output_body(counts, add, middle, own, got, out, wide):
    def read(rows, slot):
        i = rows.start // LANES
        live = jnp.where(counts[0, slot[4]] > slot[5], 1.0, 0.0)
        return live * (part_of(middle, i) + (part_of(own, i) + part_of(got, i) + row(add)))

    gather(read, wide, out)
    out.send()


def swap(value):
    return lax.ppermute(value, TENSOR, [(0, 1), (1, 0)])


def exchange(value, bits, shards):
    cores = len(bits)
    pairs = [(i * cores + core, (i ^ bit) * cores + core) for i in range(shards) for core, bit in enumerate(bits)]
    return lax.ppermute(value, (DP, TENSOR), pairs)


def per_device(
    shards,
    tokens,
    counts,
    cotangent,
    ln1_gain,
    ln1_bias,
    qkv_weight,
    qv_bias,
    out_weight,
    out_bias,
    ln2_gain,
    ln2_bias,
    up_weight,
    up_bias,
    down_weight,
    down_bias,
):
    dim = tokens.shape[1]
    width = qkv_weight.shape[2]
    units = up_weight.shape[1]
    weights = jnp.transpose(qkv_weight, (1, 0, 2))
    me = lax.axis_index(DP).astype(jnp.int32)
    place = jnp.stack([me, lax.axis_index(TENSOR).astype(jnp.int32)])
    ordered = shards == 16
    have, pieces, last = types.SimpleNamespace(), {}, [None]

    def plan_of(kernel):
        piece, cols, bits = PIECES[kernel]
        return [(Order(shards, bits) if ordered else None, cols)]

    def tied(value):
        if last[0] is None:
            return value
        return lax.optimization_barrier((value, last[0]))[0]

    def ran(outs):
        last[0] = outs[0]
        return outs

    def leave(kernel, outs):
        piece, _, bits = PIECES[kernel]
        ran(outs)
        if ordered:
            send, keep = outs
            pieces[piece] = (exchange(send, [way[0] for way in bits], shards), keep, bits)
        else:
            pieces[piece] = outs[0]

    parts = PADDED // LANES
    wide = ((WIDE, dim), F32)

    def attend_plan(kind):
        plan = [(dst, length, room, dst - kind * SPLIT) for _, length, dst, room, k, _ in SLOTS if k == kind]
        count = sum(p[2] for p in plan)
        return plan, [((count, width), BF, 1), ((count, LANES), F32, 1), ((count, dim), F32)]

    def kernel_a0():
        plan, results = attend_plan(0)
        fetched = [cotangent, up_weight, down_weight]
        outs = call(
            Kernel.A0,
            functools.partial(front_body, plan),
            [((PADDED, dim), BF), ((PADDED, dim), BF), ((PADDED, dim), BF, 0), ((PADDED, 3 * width), BF, 1)]
            + results
            + [((PADDED - SPLIT, 3 * width), BF), ((width, dim), BF)]
            + [(item.shape, BF) for item in fetched],
            [place, Far(tokens), Far(ln1_gain), Far(ln1_bias), Far(weights, chunks=0), Far(qv_bias)]
            + [Far(out_weight, wait=True)]
            + [Far(item, chunks=0) for item in fetched],
            scratch=[wide, ((dim, 3 * width), BF)],
            smem=1,
            sems=len(fetched) + 4,
            room=12,
        )
        have.near, have.normed, have.tok, have.qkv = outs[:4]
        have.mixed_a, have.lse_a, have.part_a, have.rest, have.out_weight = outs[4:9]
        have.cotangent, have.up, have.down = outs[9:]
        ran(outs)
        have.got_a = swap(have.part_a)

    def kernel_a1():
        plan, results = attend_plan(1)
        outs = call(
            Kernel.A1,
            functools.partial(attend_body, [(local, length, room, local) for _, length, room, local in plan]),
            results,
            [tied(have.rest), have.out_weight],
        )
        have.mixed_b, have.lse_b, have.part_b = ran(outs)
        have.got_b = swap(outs[2])

    def kernel_ct():
        outs = call(
            Kernel.CT,
            cotangent_body,
            [((PADDED, dim), BF), ((dim, PADDED), BF)],
            [counts, tied(have.cotangent)],
            scratch=[wide],
            smem=1,
        )
        have.gd, have.gd_t = ran(outs)

    def kernel_h():
        outs = call(
            Kernel.H,
            hidden_body,
            [((PADDED, dim), F32), ((PADDED, dim), BF), ((PADDED, units), BF), ((PADDED, units), F32)],
            [tied(have.near), Far(out_bias), Far(ln2_gain), Far(ln2_bias)]
            + [have.part_a, have.got_a, have.part_b, have.got_b]
            + [have.up, Far(up_bias)],
            room=8,
        )
        have.middle, have.normed_two, have.act, have.slope = outs
        ran(outs[1:])

    def kernel_h2():
        have.gh, have.gh_sum = ran(
            call(
                Kernel.H2,
                hidden_back_body,
                [((PADDED, units), BF), ((1, units), F32)],
                [tied(have.gd), have.slope, have.down],
            )
        )

    def kernel_t1():
        (have.normed_t,) = ran(call(Kernel.T1, transpose_body, [((dim, PADDED), BF)], [tied(have.normed)]))

    def kernel_t2():
        (have.normed_two_t,) = ran(call(Kernel.T2, transpose_body, [((dim, PADDED), BF)], [tied(have.normed_two)]))

    def kernel_g(kernel, left_t, right, first, cols):
        plan = plan_of(kernel)
        outs = call(
            kernel,
            functools.partial(gradient_body, plan, first),
            emitted(dim, plan),
            [place, tied(left_t), right],
            scratch=[((dim, cols), F32)],
            smem=1,
            room=3,
        )
        leave(kernel, outs)

    def kernel_ub():
        outs = call(
            Kernel.UB,
            up_back_body,
            [((SPLIT, dim), F32), ((PADDED - SPLIT, dim), F32)],
            [tied(have.gh), have.up],
            room=8,
        )
        have.up_a, have.up_b = ran(outs)
        have.got_up_a, have.got_up_b = swap(have.up_a), swap(have.up_b)

    def kernel_dn():
        (have.part_out,) = ran(
            call(
                Kernel.DN,
                down_body,
                [((PADDED, dim), F32)],
                [tied(have.act), Far(down_weight)],
                room=8,
            )
        )
        have.got_out = swap(have.part_out)

    def kernel_mb():
        outs = call(
            Kernel.MB,
            mid_back_body,
            [((PADDED, dim), F32, parts), ((dim, PADDED), BF), ((PADDED, width), BF), ((8, dim), F32)],
            [Far(ln2_gain), tied(have.up_a), have.got_up_a, have.up_b, have.got_up_b]
            + [have.middle, have.gd, have.out_weight],
            scratch=[((PADDED, dim), BF)],
            room=12,
        )
        have.grad_middle, have.attended_t, have.gm, have.sums_two = outs
        ran(outs[1:])

    def kernel_ab():
        plan = []
        for _, length, dst, room, kind, _ in SLOTS:
            plan.append((dst, length, room, kind, dst - kind * SPLIT))
        outs = call(
            Kernel.AB,
            functools.partial(attend_back_body, plan),
            [((PADDED, 3 * width), BF), ((8, 3 * width), F32)],
            [Far(tied(have.qkv)), Far(have.mixed_a), Far(have.mixed_b), Far(have.lse_a), Far(have.lse_b), have.gm],
            scratch=[((LANES, PADDED), F32), ((LANES, PADDED), F32)],
            room=8,
        )
        have.grads, have.sums_qkv = ran(outs)

    def kernel_qa():
        plan = plan_of(Kernel.QA)
        outs = call(
            Kernel.QA,
            functools.partial(out_and_query_body, plan, width),
            emitted(dim, plan),
            [place, tied(have.attended_t), Far(have.mixed_a), Far(have.mixed_b), have.normed_t, have.grads],
            scratch=[((PADDED, width), BF), ((dim, 2 * width), F32)],
            smem=1,
            room=3,
        )
        leave(Kernel.QA, outs)

    def kernel_nb():
        (have.part_n,) = ran(
            call(
                Kernel.NB,
                normed_back_body,
                [((PADDED, dim), F32)],
                [tied(have.grads), Far(weights, chunks=0)],
                scratch=[((dim, 3 * width), BF)],
                sems=3,
                room=6,
            )
        )
        have.got_n = swap(have.part_n)

    def kernel_out():
        (have.output,) = ran(
            call(
                Kernel.OUT,
                output_body,
                [((ROWS, dim), BF, 1)],
                [counts, Far(down_bias), tied(have.middle), have.part_out, have.got_out],
                scratch=[wide],
                smem=1,
                room=10,
            )
        )

    def kernel_ib():
        outs = call(
            Kernel.IB,
            input_back_body,
            [((ROWS, dim), BF, 1), ((16, dim), F32)],
            [Far(ln1_gain), Far(have.tok, parts), tied(have.part_n), have.got_n, Far(have.grad_middle, parts)]
            + [have.sums_two, have.sums_qkv, have.gh_sum],
            scratch=[wide],
            room=11,
        )
        have.input_grad, small = ran(outs)
        first = [way[0] for way in PIECES[Kernel.QB][2]]
        pieces[Piece.S] = (exchange(small, first, shards), small) if ordered else lax.psum(small, DP)

    kernels = {
        Kernel.A0: kernel_a0,
        Kernel.A1: kernel_a1,
        Kernel.CT: kernel_ct,
        Kernel.T1: kernel_t1,
        Kernel.H: kernel_h,
        Kernel.H2: kernel_h2,
        Kernel.T2: kernel_t2,
        Kernel.GA: lambda: kernel_g(Kernel.GA, have.gd_t, have.act, 0, units),
        Kernel.GB: lambda: kernel_g(Kernel.GB, have.normed_two_t, have.gh, 0, units),
        Kernel.QB: lambda: kernel_g(Kernel.QB, have.normed_t, have.grads, width, 2 * width),
        Kernel.UB: kernel_ub,
        Kernel.DN: kernel_dn,
        Kernel.MB: kernel_mb,
        Kernel.AB: kernel_ab,
        Kernel.QA: kernel_qa,
        Kernel.NB: kernel_nb,
        Kernel.IB: kernel_ib,
        Kernel.OUT: kernel_out,
    }

    def add(piece, step):
        if piece is Piece.S:
            got, own = pieces[piece]
            pieces[piece] = last[0] = tied(got) + own
            return
        got, keep, bits = pieces[piece]
        got = tied(got)
        ridden = piece is Piece.QB
        if ridden and step > 0:
            got, vectors = got[: keep.shape[0]], got[keep.shape[0] :]
            pieces[Piece.S] = pieces[Piece.S] + vectors
        if step == 3:
            pieces[piece] = last[0] = got + keep
            return
        half = got.shape[0] // 2
        send, keep = got[half:] + keep[half:], got[:half] + keep[:half]
        if ridden:
            send = jnp.concatenate([send, pieces[Piece.S]])
        last[0] = send
        pieces[piece] = (exchange(send, [way[step + 1] for way in bits], shards), keep, bits)

    for turn in TURNS:
        if turn in kernels:
            kernels[turn]()
        elif ordered:
            add(*turn)

    grads = [pieces[piece] for piece in (Piece.GA, Piece.GB, Piece.QA, Piece.QB)]
    if not ordered:
        grads = [lax.psum_scatter(item, DP, scatter_dimension=0, tiled=True) for item in grads]
    down_grad, up_grad = grads[:2]
    out_grad = grads[2][:, :width]
    qkv_grad = jnp.stack([grads[2][:, width:], grads[3][:, :width], grads[3][:, width:]])
    small = pieces[Piece.S]
    mine = lax.dynamic_slice_in_dim(small[:6], me * (dim // shards), dim // shards, 1)
    rest = small[6:9].reshape(-1)
    return (
        have.output,
        have.input_grad,
        mine[0],
        mine[1],
        jnp.transpose(qkv_grad, (1, 0, 2)),
        rest[: 2 * width].reshape(2, width),
        out_grad.T,
        mine[2],
        mine[3],
        mine[4],
        up_grad,
        rest[2 * width :],
        down_grad.T,
        mine[5],
    )


def solution(mesh):
    in_specs = (
        P(DP, None),
        P(DP, None),
        P(DP, None),
        P(),
        P(),
        P(None, None, TENSOR),
        P(None, TENSOR),
        P(TENSOR, None),
        P(),
        P(),
        P(),
        P(None, TENSOR),
        P(TENSOR),
        P(TENSOR, None),
        P(),
    )
    out_specs = (
        P(DP, None),
        P(DP, None),
        P(DP),
        P(DP),
        P(DP, None, TENSOR),
        P(None, TENSOR),
        P(TENSOR, DP),
        P(DP),
        P(DP),
        P(DP),
        P(DP, TENSOR),
        P(TENSOR),
        P(TENSOR, DP),
        P(DP),
    )
    return jax.shard_map(
        functools.partial(per_device, mesh.shape[DP]),
        mesh=mesh,
        in_specs=in_specs,
        out_specs=out_specs,
        check_vma=False,
    )
```

```python
import enum
import functools
import math
import types

import jax
import jax.numpy as jnp
from jax import lax
from jax.experimental import pallas as pl
from jax.experimental.pallas import tpu as pltpu
from jax.sharding import PartitionSpec as P

HEAD_DIM = 64
LONG_LEN = 608
SHORT_LEN = 228
LONG_SLOTS = 1
SHORT_SLOTS = 2
EPS = 1e-06

DP, TENSOR = "dp", "tensor"
LANES = 128
PAIR = 2 * HEAD_DIM
BF = jnp.bfloat16
F32 = jnp.float32
VMEM_LIMIT = 60 * 1024 * 1024


def up_to(value, unit):
    return -(-value // unit) * unit


def slots():
    found, src, dst = [], 0, 0
    for kind, (number, length) in enumerate(((LONG_SLOTS, LONG_LEN), (SHORT_SLOTS, SHORT_LEN))):
        for index in range(number):
            room = up_to(length, LANES)
            found.append((src, length, dst, room, kind, index))
            src, dst = src + length, dst + room
    return found, src, dst


SLOTS, ROWS, PADDED = slots()
SPLIT = sum(slot[3] for slot in SLOTS if slot[4] == 0)
CHUNK = PADDED // 3


def row(ref):
    return ref[...].reshape(1, -1)


def nn(left, right):
    return lax.dot_general(left, right, (((1,), (0,)), ((), ())), preferred_element_type=F32)


def nt(left, right):
    return lax.dot_general(left, right, (((1,), (1,)), ((), ())), preferred_element_type=F32)


NAMES = ("A0", "A1", "CT", "T1", "H", "H2", "T2", "GA", "GB", "UB", "DN", "MB", "AB", "QA", "QB", "NB", "IB", "OUT")
Kernel = enum.Enum("Kernel", NAMES)
Piece = enum.Enum("Piece", ("GA", "GB", "QA", "QB", "S"))
K, P_ = Kernel, Piece
TURNS = [
    K.A0, K.A1, K.CT, K.T1, K.H, K.GA, K.H2, K.T2, K.GB, K.UB, K.MB, (P_.GA, 0), K.AB, K.NB, (P_.GA, 1), K.QA,
    (P_.GB, 0), (P_.GA, 2), K.QB, K.IB, K.DN, (P_.GB, 1), (P_.S, 0), (P_.QA, 0), (P_.QB, 0), (P_.GB, 2), (P_.QB, 1),
    (P_.GA, 3), (P_.QA, 1), (P_.QB, 2), (P_.GB, 3), (P_.QA, 2), K.OUT, (P_.QB, 3), (P_.QA, 3),
]
PIECES = {
    K.GA: (P_.GA, 1536, ((2, 1, 4, 8), (4, 8, 2, 1))),
    K.GB: (P_.GB, 1536, ((2, 4, 1, 8), (1, 2, 4, 8))),
    K.QA: (P_.QA, 768, ((1, 4, 2, 8), (1, 2, 4, 8))),
    K.QB: (P_.QB, 768, ((4, 2, 1, 8), (2, 1, 4, 8))),
}
COSTS = {
    K.A1: 1000000000,
    K.UB: 10000000000,
    K.AB: 10000000000,
    K.A0: 3000000000,
    K.OUT: 1000000000,
    K.H: 1000000000,
    K.CT: 1000000000,
    K.T2: 1000000000,
    K.IB: 3000000000,
    K.T1: 1000000000,
    K.NB: 1000000000,
    K.QA: 10000000000,
    K.H2: 1000000000,
    K.GA: 1000000000,
    K.GB: 3000000000,
    K.MB: 1000000000,
    K.DN: 1000000000,
    K.QB: 3000000000,
}


def held(shape, dtype):
    shape = (1, *shape)
    lead = math.prod(shape[:-2])
    return lead * up_to(shape[-2], 16) * up_to(shape[-1], LANES) * jnp.dtype(dtype).itemsize


class Far:
    def __init__(self, value, chunks=1, rows=None, cols=None, wait=False):
        self.value, self.chunks, self.rows, self.cols, self.wait = value, chunks, rows, cols, wait

    @property
    def shape(self):
        shape = list(self.value.shape)
        if self.rows is not None:
            shape[0] = self.rows[1]
        if self.cols is not None:
            shape[-1] = self.cols[1]
        return tuple(shape)

    @property
    def dtype(self):
        return self.value.dtype


class Late:
    def __init__(self, spec, source, buffer, sems):
        self.buffer, self.left = buffer, {}
        if spec.rows is not None:
            source = source.at[pl.ds(*spec.rows)]
        if spec.cols is not None:
            source = source.at[..., pl.ds(*spec.cols)]
        size = spec.shape[0] // spec.chunks
        for i in range(spec.chunks):
            parts = (source, buffer)
            if spec.chunks > 1:
                parts = (ref.at[i * size : (i + 1) * size] for ref in parts)
            self.left[i] = pltpu.make_async_copy(*parts, sems.at[i])
        if not spec.wait:
            self.start()

    def start(self):
        for copy in self.left.values():
            copy.start()

    def rows(self, i):
        if i in self.left:
            self.left.pop(i).wait()
        return self.buffer

    def all(self):
        for i in list(self.left):
            self.rows(i)
        return self.buffer

    @property
    def shape(self):
        return self.buffer.shape

    def __getitem__(self, key):
        return self.all()[key]


def part_of(ref, i):
    rows = slice(i * LANES, (i + 1) * LANES)
    return ref.rows(i)[rows, :] if isinstance(ref, Late) else ref[rows, :]


class Away:
    def __init__(self, buffer, target, sems, chunks):
        self.buffer, self.target, self.sems, self.chunks, self.sent = buffer, target, sems, chunks, []

    @property
    def shape(self):
        return self.buffer.shape

    def __setitem__(self, key, value):
        self.buffer[key] = value

    def __getitem__(self, key):
        return self.buffer[key]

    def send(self, i=None):
        parts = (self.buffer, self.target)
        if i is not None:
            size = self.buffer.shape[0] // self.chunks
            parts = (ref.at[i * size : (i + 1) * size] for ref in parts)
        copy = pltpu.make_async_copy(*parts, self.sems.at[i or 0])
        copy.start()
        self.sent.append(copy)


def call(kernel, body, outs, args, scratch=(), smem=0, sems=0, room=4):
    specs = [pl.BlockSpec(memory_space=pltpu.SMEM)] * smem
    buffers = []
    for arg in args[smem:]:
        far = isinstance(arg, Far)
        specs.append(pl.BlockSpec(memory_space=pl.ANY if far else pltpu.VMEM))
        if far:
            if arg.chunks:
                buffers += [pltpu.VMEM(arg.shape, arg.dtype), pltpu.SemaphoreType.DMA((arg.chunks,))]
    for out in outs:
        if len(out) > 2 and out[2]:
            buffers += [pltpu.VMEM(out[0], out[1]), pltpu.SemaphoreType.DMA((out[2],))]
    need = sum(held(*item[:2]) for item in [*(out for out in outs if len(out) > 2 and out[2]), *scratch])
    need += sum(held(arg.shape, arg.dtype) for arg in args[smem:] if isinstance(arg, Far) and arg.chunks)
    spaces = [pltpu.SMEM] * smem + [pltpu.HBM if isinstance(arg, Far) else pltpu.VMEM for arg in args[smem:]]
    values = [arg.value if isinstance(arg, Far) else arg for arg in args]
    values[smem:] = [pltpu.with_memory_space_constraint(*pair) for pair in zip(values[smem:], spaces[smem:])]

    def run(*refs):
        given, refs = refs[: len(args)], refs[len(args) :]
        made, refs = refs[: len(outs)], refs[len(outs) :]
        count = len(scratch) + (1 if sems else 0)
        own, extra = refs[:count], list(refs[count:])
        ins, results = [], []
        for arg, ref in zip(args, given):
            late = isinstance(arg, Far) and arg.chunks
            ins.append(Late(arg, ref, extra.pop(0), extra.pop(0)) if late else ref)
        for out, ref in zip(outs, made):
            away = len(out) > 2 and out[2]
            results.append(Away(extra.pop(0), ref, extra.pop(0), out[2]) if away else ref)
        body(*ins, *results, *own)
        for item in ins:
            if isinstance(item, Late):
                item.all()
        for item in results:
            if isinstance(item, Away):
                for copy in item.sent:
                    copy.wait()

    return pl.pallas_call(
        run,
        out_shape=[pltpu.HBM(*out[:2]) if len(out) > 2 else pltpu.VMEM(*out) for out in outs],
        in_specs=specs,
        out_specs=[pl.BlockSpec(memory_space=pl.ANY if len(out) > 2 else pltpu.VMEM) for out in outs],
        scratch_shapes=[pltpu.VMEM(*item) for item in scratch]
        + ([pltpu.SemaphoreType.DMA((sems,))] if sems else [])
        + buffers,
        compiler_params=pltpu.CompilerParams(vmem_limit_bytes=need + room * 2**20),
        cost_estimate=pl.CostEstimate(flops=COSTS.get(kernel, 1000), bytes_accessed=1000, transcendentals=0),
        name=kernel.name.lower(),
    )(*values)


def row_loop(step, body, rows=PADDED):
    def run(i, carry):
        body(pl.ds(pl.multiple_of(i * step, step), step))
        return carry

    lax.fori_loop(0, rows // step, run, 0)


def normal_parts(values):
    center = values - jnp.mean(values, axis=-1, keepdims=True)
    spread = jnp.mean(center * center, axis=-1, keepdims=True)
    ratio = lax.rsqrt(spread + EPS)
    return center * ratio, ratio


def norm_back(values, gain, grad):
    hat, ratio = normal_parts(values)
    scaled = grad * gain
    mean_one = jnp.mean(scaled, axis=-1, keepdims=True)
    mean_two = jnp.mean(scaled * hat, axis=-1, keepdims=True)
    back = ratio * (scaled - mean_one - hat * mean_two)
    return back, jnp.sum(grad * hat, axis=0, keepdims=True), jnp.sum(grad, axis=0, keepdims=True)


def spread(source, wide, write):
    wide[:ROWS, :] = source[...].astype(F32)
    for slot in SLOTS:
        src, length, dst, room = slot[:4]
        for i in range(0, room, LANES):
            values = wide[src + i : src + i + LANES, :]
            if i + LANES > length:
                row = lax.broadcasted_iota(jnp.int32, values.shape, 0)
                values = jnp.where(row < length - i, values, 0.0)
            write(slice(dst + i, dst + i + LANES), values, slot)


def gather(read, wide, target):
    for slot in SLOTS:
        src, _, dst, room = slot[:4]
        for i in range(0, room, LANES):
            wide[src + i : src + i + LANES, :] = read(slice(dst + i, dst + i + LANES), slot)
    target[...] = wide[:ROWS, :].astype(BF)


WIDE = up_to(ROWS + LANES, LANES)


def project_body(tokens, gain, shift, weight, bias, tok, normed, qkv, wide, copies):
    width = weight.shape[1] // 3
    scale = HEAD_DIM ** (-0.5)

    def write(rows, values, slot):
        tok[rows, :] = values.astype(BF)
        hat, _ = normal_parts(values)
        normed[rows, :] = (hat * row(gain) + row(shift)).astype(BF)

    spread(tokens, wide, write)
    for copy in copies:
        copy.wait()
    for start in range(0, PADDED, CHUNK):
        rows = slice(start, start + CHUNK)
        proj = nn(normed[rows, :], weight[...])
        qkv[rows, :width] = ((proj[:, :width] + bias[0:1, :]) * scale).astype(BF)
        qkv[rows, width : 2 * width] = proj[:, width : 2 * width].astype(BF)
        qkv[rows, 2 * width :] = (proj[:, 2 * width :] + bias[1:2, :]).astype(BF)
    qkv.send()


UNIT = 256


def head_mask(rows, which):
    lane = lax.broadcasted_iota(jnp.int32, (rows, PAIR), 1)
    return (lane // HEAD_DIM) == which


def both_heads(block):
    zero = jnp.zeros_like(block)
    return jnp.concatenate([jnp.where(head_mask(block.shape[0], which), block, zero) for which in range(2)])


def join_heads(block):
    half = block.shape[0] // 2
    return jnp.where(head_mask(half, 0), block[:half], block[half:])


def attend_body(plan, qkv, out_weight, mixed, lse, part):
    width = qkv.shape[1] // 3
    for start, length, room, local in plan:
        lane = lax.broadcasted_iota(jnp.int32, (room, LANES), 1)
        keep = lax.broadcasted_iota(jnp.int32, (1, room), 1) < length
        stats = jnp.zeros((room, LANES), F32)

        def scores_of(pair):
            q, k = (qkv[start : start + room, at : at + PAIR] for at in (pair * PAIR, width + pair * PAIR))
            return jnp.where(keep, nt(both_heads(q), k), -1e30)

        scores = scores_of(0)
        for pair in range(width // PAIR):
            later = scores_of(pair + 1) if pair + 1 < width // PAIR else None
            v = qkv[start : start + room, 2 * width + pair * PAIR : 2 * width + (pair + 1) * PAIR]
            top = jnp.max(scores, axis=-1, keepdims=True)
            expo = jnp.exp(scores - top)
            total = jnp.sum(expo, axis=-1, keepdims=True)
            out = nn(expo.astype(BF), v) / total
            mixed[local : local + room, pair * PAIR : (pair + 1) * PAIR] = join_heads(out).astype(BF)
            log_total = top + jnp.log(total)
            stats = jnp.where(lane == 2 * pair, log_total[:room], stats)
            stats = jnp.where(lane == 2 * pair + 1, log_total[room:], stats)
            scores = later
        lse[local : local + room, :] = stats
    mixed.send()
    lse.send()
    part[...] = nn(mixed[...], out_weight[...])


def front_body(plan, me, tokens, gain, shift, weight, bias, out_weight, *refs):
    count = (len(refs) - 12) // 2
    fetched, (tok, normed, tok_far), (qkv, mixed, lse, part, rest, kept) = refs[:count], refs[count:][:3], refs[count + 3 :][:6]
    targets, (wide, flat, sems) = refs[count + 9 : -3], refs[-3:]
    width = flat.shape[1] // 3
    first = []
    for n in range(3):
        first.append(pltpu.make_async_copy(weight.at[n], flat.at[:, n * width : (n + 1) * width], sems.at[n]))
        first[n].start()
    copies = [pltpu.make_async_copy(*pair, sems.at[3 + n]) for n, pair in enumerate(zip(fetched, targets))]
    copies.append(pltpu.make_async_copy(tok, tok_far, sems.at[3 + count]))
    project_body(tokens, gain, shift, flat, bias, tok, normed, qkv, wide, first)
    out_weight.start()
    for copy in copies:
        copy.start()
    rest[...] = qkv[SPLIT:, :]
    attend_body(plan, qkv, out_weight, mixed, lse, part)
    kept[...] = out_weight[...]
    for copy in copies:
        copy.wait()


def hidden_body(tok, add, gain, shift, own_a, got_a, own_b, got_b, up, up_add, middle, normed, act, slope):
    for i in range(PADDED // LANES):
        rows = slice(i * LANES, (i + 1) * LANES)
        base, own, got = (0, own_a, got_a) if i < SPLIT // LANES else (SPLIT, own_b, got_b)
        n = i - base // LANES
        mid = part_of(tok, i).astype(F32) + (part_of(own, n) + part_of(got, n) + row(add))
        middle[rows, :] = mid
        hat, _ = normal_parts(mid)
        normed[rows, :] = (hat * row(gain) + row(shift)).astype(BF)
    for start in range(0, PADDED, CHUNK):
        rows = slice(start, start + CHUNK)
        for col in range(0, act.shape[1], UNIT):
            cols = slice(col, col + UNIT)
            hidden = nn(normed[rows, :], up[:, cols]) + row(up_add)[:, cols]
            cdf = 0.5 + 0.5 * lax.erf(hidden * (2.0**-0.5))
            act[rows, cols] = (hidden * cdf).astype(BF)
            slope[rows, cols] = cdf + hidden * (jnp.exp(hidden * hidden * -0.5) * ((2.0 * math.pi) ** -0.5))


def hidden_back_body(gd, slope, down, gh, gh_sum):
    for start in range(0, PADDED, CHUNK):
        rows = slice(start, start + CHUNK)
        for col in range(0, gh.shape[1], UNIT):
            cols = slice(col, col + UNIT)
            gh[rows, cols] = (nt(gd[rows, :], down[cols, :]) * slope[rows, cols]).astype(BF)
    gh_sum[...] = jnp.sum(gh[...].astype(F32), axis=0, keepdims=True)


def transpose_body(source, target):
    source = source.all() if isinstance(source, Late) else source
    def step(rows):
        target[:, rows] = source[rows, :].astype(F32).T.astype(BF)

    row_loop(LANES, step, source.shape[0])


def cotangent_body(counts, cotangent, gd, gd_t, wide):
    def write(rows, values, slot):
        live = jnp.where(counts[0, slot[4]] > slot[5], 1.0, 0.0)
        values = values * live
        gd[rows, :] = values.astype(BF)
        gd_t[:, rows] = values.T.astype(BF)

    spread(cotangent, wide, write)


class Order:
    def __init__(self, shards, bits):
        self.shards, self.bits = shards, bits

    def shard(self, place, core):
        count = len(self.bits[0])
        found = [sum(bit for n, bit in enumerate(bits) if (place >> (count - 1 - n)) & 1) for bits in self.bits]
        return jnp.where(core == 0, *found)


def store_ordered(scratch, me, order, col, width, send, keep):
    size = scratch.shape[0] // order.shards
    half = order.shards // 2
    for place in range(order.shards):
        source = pl.ds(pl.multiple_of((me[0] ^ order.shard(place, me[1])) * size, size), size)
        target, base = (keep, place) if place < half else (send, place - half)
        target[base * size : (base + 1) * size, :] = scratch[source, col : col + width]


def hand_out(scratch, me, plan, refs):
    col = 0
    for n, (order, width) in enumerate(plan):
        if order is None:
            refs[n][...] = scratch[:, col : col + width]
        else:
            store_ordered(scratch, me, order, col, width, refs[2 * n], refs[2 * n + 1])
        col += width


def emitted(dim, plan):
    outs = []
    for order, width in plan:
        if order is None:
            outs.append(((dim, width), F32))
        else:
            outs += [((dim // 2, width), F32)] * 2
    return outs


def in_chunks(out, product):
    for start in range(0, PADDED, CHUNK):
        rows = slice(start, start + CHUNK)
        out[rows, :] = product(rows)


def up_back_body(left, right, out_a, out_b):
    out_a[...] = nt(left[:SPLIT, :], right[...])
    out_b[...] = nt(left[SPLIT:, :], right[...])


def down_body(left, right, out):
    in_chunks(out, lambda rows: nn(left[rows, :], right[...]))


def mid_back_body(gain, own_a, got_a, own_b, got_b, middle, gd, out_weight, grad_middle, attended_t, gm, sums, attended):
    total = jnp.zeros(sums.shape, F32)
    for i in range(PADDED // LANES):
        rows = slice(i * LANES, (i + 1) * LANES)
        grad_out = gd[rows, :].astype(F32)
        base, own, got = (0, own_a, got_a) if i < SPLIT // LANES else (SPLIT, own_b, got_b)
        grad = part_of(own, i - base // LANES) + part_of(got, i - base // LANES)
        back, gain_sum, shift_sum = norm_back(part_of(middle, i), row(gain), grad)
        whole = grad_out + back
        grad_middle[rows, :] = whole
        grad_middle.send(i)
        short = whole.astype(BF)
        wide = short.astype(F32)
        attended[rows, :] = short
        attended_t[:, rows] = wide.T.astype(BF)
        parts = [gain_sum, shift_sum, jnp.sum(wide, axis=0, keepdims=True), jnp.sum(grad_out, axis=0, keepdims=True)]
        total += jnp.concatenate(parts + [jnp.zeros((4, wide.shape[1]), F32)])
    sums[...] = total
    gm[...] = nt(attended[...], out_weight[...]).astype(BF)


def attend_back_body(plan, qkv, mixed_a, mixed_b, lse_a, lse_b, gm, grads, sums, stats_t, delta_t):
    width = qkv.shape[1] // 3
    heads = width // HEAD_DIM
    scale = HEAD_DIM ** (-0.5)
    for start, length, room, part, offset in plan:
        mixed, lse = ((mixed_a, lse_a), (mixed_b, lse_b))[part]
        for i in range(room // LANES):
            at = slice(start + i * LANES, start + (i + 1) * LANES)
            loc = slice(offset + i * LANES, offset + (i + 1) * LANES)
            stats_t[:, at] = lse[loc, :].T
            lane = lax.broadcasted_iota(jnp.int32, (LANES, LANES), 1)
            delta = jnp.zeros((LANES, LANES), F32)
            for head in range(heads):
                pair = slice(head // 2 * PAIR, (head // 2 + 1) * PAIR)
                prod = gm[at, pair].astype(F32) * mixed[loc, pair].astype(F32)
                one = jnp.sum(jnp.where(head_mask(LANES, head % 2), prod, 0.0), axis=-1, keepdims=True)
                delta = jnp.where(lane == head, one, delta)
            delta_t[:, at] = delta.T
        tall = up_to(length, 16)
        valid = lax.broadcasted_iota(jnp.int32, (tall, room), 0) < length
        for pair in range(heads // 2):
            cols = slice(pair * PAIR, (pair + 1) * PAIR)
            q = qkv[start : start + room, cols]
            k = qkv[start : start + tall, width + pair * PAIR : width + (pair + 1) * PAIR]
            v = qkv[start : start + tall, 2 * width + pair * PAIR : 2 * width + (pair + 1) * PAIR]
            do = gm[start : start + room, cols]
            k_t = k.astype(F32).T.astype(BF)
            scores = nt(both_heads(k), q)
            grad_probs = nt(both_heads(v), do)
            probs, grad_scores, grad_q = [], [], []
            for which in range(2):
                head = 2 * pair + which
                at = slice(which * tall, (which + 1) * tall)
                prob = jnp.exp(scores[at] - stats_t[head : head + 1, start : start + room])
                if tall != length:
                    prob = jnp.where(valid, prob, 0.0)
                grad = (prob * (grad_probs[at] - delta_t[head : head + 1, start : start + room])).astype(BF)
                probs.append(prob.astype(BF))
                grad_scores.append(grad)
                grad_q.append(nn(k_t[which * HEAD_DIM : (which + 1) * HEAD_DIM, :], grad))
            grad_v = join_heads(nn(jnp.concatenate(probs), do))
            grad_k = join_heads(nn(jnp.concatenate(grad_scores), q))
            turned = jnp.concatenate(grad_q, axis=0).T
            grads[start : start + room, cols] = (turned.astype(BF).astype(F32) * scale).astype(BF)
            for base, value in ((width, grad_k), (2 * width, grad_v)):
                at = slice(base + pair * PAIR, base + (pair + 1) * PAIR)
                grads[start : start + tall, at] = value.astype(BF)
                if tall != room:
                    grads[start + tall : start + room, at] = jnp.zeros((room - tall, PAIR), BF)
    sums[0:1, :] = jnp.sum(grads[...].astype(F32), axis=0, keepdims=True)


def normed_back_body(grads, weight, out, flat, sems):
    width = flat.shape[1] // 3
    copies = []
    for n in range(3):
        copies.append(pltpu.make_async_copy(weight.at[n], flat.at[:, n * width : (n + 1) * width], sems.at[n]))
        copies[n].start()
    for copy in copies:
        copy.wait()
    in_chunks(out, lambda rows: nt(grads[rows, :], flat[...]))


def gradient_body(plan, first, me, left_t, right, *refs):
    scratch = refs[-1]
    for col in range(0, scratch.shape[1], 256):
        scratch[:, col : col + 256] = nn(left_t[...], right[:, first + col : first + col + 256])
    hand_out(scratch, me, plan, refs[:-1])


def out_and_query_body(plan, query, me, attended_t, mixed_a, mixed_b, normed_t, grads, *refs):
    mixed, scratch = refs[-2:]
    mixed[:SPLIT, :] = mixed_a[...]
    mixed[SPLIT:, :] = mixed_b[...]
    width = mixed.shape[1]
    scratch[:, :width] = nn(attended_t[...], mixed[...])
    scratch[:, width:] = nn(normed_t[...], grads[:, :query])
    hand_out(scratch, me, plan, refs[:-2])


def input_back_body(gain, tok, own, got, grad_middle, sums_two, sums_qkv, gh_sum, grad, small, wide):
    totals = [jnp.zeros((1, grad.shape[1]), F32)] * 2

    def read(rows, slot):
        i = rows.start // LANES
        back, *sums = norm_back(part_of(tok, i).astype(F32), row(gain), part_of(own, i) + part_of(got, i))
        totals[:] = [total + item for total, item in zip(totals, sums)]
        return part_of(grad_middle, i) + back

    gather(read, wide, grad)
    grad.send()
    width = sums_qkv.shape[1] // 3
    qv = jnp.concatenate([sums_qkv[0:1, :width], sums_qkv[0:1, 2 * width :]], axis=1)
    two = [sums_two[n : n + 1, :] for n in (2, 0, 1, 3)]
    small[...] = jnp.zeros_like(small)
    for n, item in enumerate([*totals, *two, qv, gh_sum[:, : grad.shape[1]], gh_sum[:, grad.shape[1] :]]):
        small[n : n + 1, :] = item


def output_body(counts, add, middle, own, got, out, wide):
    def read(rows, slot):
        i = rows.start // LANES
        live = jnp.where(counts[0, slot[4]] > slot[5], 1.0, 0.0)
        return live * (part_of(middle, i) + (part_of(own, i) + part_of(got, i) + row(add)))

    gather(read, wide, out)
    out.send()


def swap(value):
    return lax.ppermute(value, TENSOR, [(0, 1), (1, 0)])


def exchange(value, bits, shards):
    cores = len(bits)
    pairs = [(i * cores + core, (i ^ bit) * cores + core) for i in range(shards) for core, bit in enumerate(bits)]
    return lax.ppermute(value, (DP, TENSOR), pairs)


def per_device(
    shards,
    tokens,
    counts,
    cotangent,
    ln1_gain,
    ln1_bias,
    qkv_weight,
    qv_bias,
    out_weight,
    out_bias,
    ln2_gain,
    ln2_bias,
    up_weight,
    up_bias,
    down_weight,
    down_bias,
):
    dim = tokens.shape[1]
    width = qkv_weight.shape[2]
    units = up_weight.shape[1]
    weights = jnp.transpose(qkv_weight, (1, 0, 2))
    me = lax.axis_index(DP).astype(jnp.int32)
    place = jnp.stack([me, lax.axis_index(TENSOR).astype(jnp.int32)])
    ordered = shards == 16
    have, pieces, last = types.SimpleNamespace(), {}, [None]

    def plan_of(kernel):
        piece, cols, bits = PIECES[kernel]
        return [(Order(shards, bits) if ordered else None, cols)]

    def tied(value):
        if last[0] is None:
            return value
        return lax.optimization_barrier((value, last[0]))[0]

    def ran(outs):
        last[0] = outs[0]
        return outs

    def leave(kernel, outs):
        piece, _, bits = PIECES[kernel]
        ran(outs)
        if ordered:
            send, keep = outs
            pieces[piece] = (exchange(send, [way[0] for way in bits], shards), keep, bits)
        else:
            pieces[piece] = outs[0]

    parts = PADDED // LANES
    wide = ((WIDE, dim), F32)

    def attend_plan(kind):
        plan = [(dst, length, room, dst - kind * SPLIT) for _, length, dst, room, k, _ in SLOTS if k == kind]
        count = sum(p[2] for p in plan)
        return plan, [((count, width), BF, 1), ((count, LANES), F32, 1), ((count, dim), F32)]

    def kernel_a0():
        plan, results = attend_plan(0)
        fetched = [cotangent, up_weight, down_weight, out_bias, ln2_gain, ln2_bias, up_bias]
        outs = call(
            Kernel.A0,
            functools.partial(front_body, plan),
            [((PADDED, dim), BF), ((PADDED, dim), BF), ((PADDED, dim), BF, 0), ((PADDED, 3 * width), BF, 1)]
            + results
            + [((PADDED - SPLIT, 3 * width), BF), ((width, dim), BF)]
            + [(item.shape, item.dtype) for item in fetched],
            [place, Far(tokens), Far(ln1_gain), Far(ln1_bias), Far(weights, chunks=0), Far(qv_bias)]
            + [Far(out_weight, wait=True)]
            + [Far(item, chunks=0) for item in fetched],
            scratch=[wide, ((dim, 3 * width), BF)],
            smem=1,
            sems=len(fetched) + 4,
            room=12,
        )
        have.near, have.normed, have.tok, have.qkv = outs[:4]
        have.mixed_a, have.lse_a, have.part_a, have.rest, have.out_weight = outs[4:9]
        have.cotangent, have.up, have.down, have.out_bias, have.gain, have.shift, have.up_bias = outs[9:]
        ran(outs)
        have.got_a = swap(have.part_a)

    def kernel_a1():
        plan, results = attend_plan(1)
        outs = call(
            Kernel.A1,
            functools.partial(attend_body, [(local, length, room, local) for _, length, room, local in plan]),
            results,
            [tied(have.rest), have.out_weight],
        )
        have.mixed_b, have.lse_b, have.part_b = ran(outs)
        have.got_b = swap(outs[2])

    def kernel_ct():
        outs = call(
            Kernel.CT,
            cotangent_body,
            [((PADDED, dim), BF), ((dim, PADDED), BF)],
            [counts, tied(have.cotangent)],
            scratch=[wide],
            smem=1,
        )
        have.gd, have.gd_t = ran(outs)

    def kernel_h():
        outs = call(
            Kernel.H,
            hidden_body,
            [((PADDED, dim), F32), ((PADDED, dim), BF), ((PADDED, units), BF), ((PADDED, units), F32)],
            [tied(have.near), have.out_bias, have.gain, have.shift]
            + [have.part_a, have.got_a, have.part_b, have.got_b]
            + [have.up, have.up_bias],
            room=8,
        )
        have.middle, have.normed_two, have.act, have.slope = outs
        ran(outs[1:])

    def kernel_h2():
        have.gh, have.gh_sum = ran(
            call(
                Kernel.H2,
                hidden_back_body,
                [((PADDED, units), BF), ((1, units), F32)],
                [tied(have.gd), have.slope, have.down],
            )
        )

    def kernel_t1():
        (have.normed_t,) = ran(call(Kernel.T1, transpose_body, [((dim, PADDED), BF)], [tied(have.normed)]))

    def kernel_t2():
        (have.normed_two_t,) = ran(call(Kernel.T2, transpose_body, [((dim, PADDED), BF)], [tied(have.normed_two)]))

    def kernel_g(kernel, left_t, right, first, cols):
        plan = plan_of(kernel)
        outs = call(
            kernel,
            functools.partial(gradient_body, plan, first),
            emitted(dim, plan),
            [place, tied(left_t), right],
            scratch=[((dim, cols), F32)],
            smem=1,
            room=3,
        )
        leave(kernel, outs)

    def kernel_ub():
        outs = call(
            Kernel.UB,
            up_back_body,
            [((SPLIT, dim), F32), ((PADDED - SPLIT, dim), F32)],
            [tied(have.gh), have.up],
            room=8,
        )
        have.up_a, have.up_b = ran(outs)
        have.got_up_a, have.got_up_b = swap(have.up_a), swap(have.up_b)

    def kernel_dn():
        (have.part_out,) = ran(
            call(
                Kernel.DN,
                down_body,
                [((PADDED, dim), F32)],
                [tied(have.act), Far(down_weight)],
                room=8,
            )
        )
        have.got_out = swap(have.part_out)

    def kernel_mb():
        outs = call(
            Kernel.MB,
            mid_back_body,
            [((PADDED, dim), F32, parts), ((dim, PADDED), BF), ((PADDED, width), BF), ((8, dim), F32)],
            [have.gain, tied(have.up_a), have.got_up_a, have.up_b, have.got_up_b]
            + [have.middle, have.gd, have.out_weight],
            scratch=[((PADDED, dim), BF)],
            room=12,
        )
        have.grad_middle, have.attended_t, have.gm, have.sums_two = outs
        ran(outs[1:])

    def kernel_ab():
        plan = []
        for _, length, dst, room, kind, _ in SLOTS:
            plan.append((dst, length, room, kind, dst - kind * SPLIT))
        outs = call(
            Kernel.AB,
            functools.partial(attend_back_body, plan),
            [((PADDED, 3 * width), BF), ((8, 3 * width), F32)],
            [Far(tied(have.qkv)), Far(have.mixed_a), Far(have.mixed_b), Far(have.lse_a), Far(have.lse_b), have.gm],
            scratch=[((LANES, PADDED), F32), ((LANES, PADDED), F32)],
            room=8,
        )
        have.grads, have.sums_qkv = ran(outs)

    def kernel_qa():
        plan = plan_of(Kernel.QA)
        outs = call(
            Kernel.QA,
            functools.partial(out_and_query_body, plan, width),
            emitted(dim, plan),
            [place, tied(have.attended_t), Far(have.mixed_a), Far(have.mixed_b), have.normed_t, have.grads],
            scratch=[((PADDED, width), BF), ((dim, 2 * width), F32)],
            smem=1,
            room=3,
        )
        leave(Kernel.QA, outs)

    def kernel_nb():
        (have.part_n,) = ran(
            call(
                Kernel.NB,
                normed_back_body,
                [((PADDED, dim), F32)],
                [tied(have.grads), Far(weights, chunks=0)],
                scratch=[((dim, 3 * width), BF)],
                sems=3,
                room=6,
            )
        )
        have.got_n = swap(have.part_n)

    def kernel_out():
        (have.output,) = ran(
            call(
                Kernel.OUT,
                output_body,
                [((ROWS, dim), BF, 1)],
                [counts, Far(down_bias), tied(have.middle), have.part_out, have.got_out],
                scratch=[wide],
                smem=1,
                room=10,
            )
        )

    def kernel_ib():
        outs = call(
            Kernel.IB,
            input_back_body,
            [((ROWS, dim), BF, 1), ((16, dim), F32)],
            [Far(ln1_gain), Far(have.tok, parts), tied(have.part_n), have.got_n, Far(have.grad_middle, parts)]
            + [have.sums_two, have.sums_qkv, have.gh_sum],
            scratch=[wide],
            room=11,
        )
        have.input_grad, small = ran(outs)
        first = [way[0] for way in PIECES[Kernel.QB][2]]
        pieces[Piece.S] = (exchange(small, first, shards), small) if ordered else lax.psum(small, DP)

    kernels = {
        Kernel.A0: kernel_a0,
        Kernel.A1: kernel_a1,
        Kernel.CT: kernel_ct,
        Kernel.T1: kernel_t1,
        Kernel.H: kernel_h,
        Kernel.H2: kernel_h2,
        Kernel.T2: kernel_t2,
        Kernel.GA: lambda: kernel_g(Kernel.GA, have.gd_t, have.act, 0, units),
        Kernel.GB: lambda: kernel_g(Kernel.GB, have.normed_two_t, have.gh, 0, units),
        Kernel.QB: lambda: kernel_g(Kernel.QB, have.normed_t, have.grads, width, 2 * width),
        Kernel.UB: kernel_ub,
        Kernel.DN: kernel_dn,
        Kernel.MB: kernel_mb,
        Kernel.AB: kernel_ab,
        Kernel.QA: kernel_qa,
        Kernel.NB: kernel_nb,
        Kernel.IB: kernel_ib,
        Kernel.OUT: kernel_out,
    }

    def add(piece, step):
        if piece is Piece.S:
            got, own = pieces[piece]
            pieces[piece] = last[0] = tied(got) + own
            return
        got, keep, bits = pieces[piece]
        got = tied(got)
        ridden = piece is Piece.QB
        if ridden and step > 0:
            got, vectors = got[: keep.shape[0]], got[keep.shape[0] :]
            pieces[Piece.S] = pieces[Piece.S] + vectors
        if step == 3:
            pieces[piece] = last[0] = got + keep
            return
        half = got.shape[0] // 2
        send, keep = got[half:] + keep[half:], got[:half] + keep[:half]
        if ridden:
            send = jnp.concatenate([send, pieces[Piece.S]])
        last[0] = send
        pieces[piece] = (exchange(send, [way[step + 1] for way in bits], shards), keep, bits)

    for turn in TURNS:
        if turn in kernels:
            kernels[turn]()
        elif ordered:
            add(*turn)

    grads = [pieces[piece] for piece in (Piece.GA, Piece.GB, Piece.QA, Piece.QB)]
    if not ordered:
        grads = [lax.psum_scatter(item, DP, scatter_dimension=0, tiled=True) for item in grads]
    down_grad, up_grad = grads[:2]
    out_grad = grads[2][:, :width]
    qkv_grad = jnp.stack([grads[2][:, width:], grads[3][:, :width], grads[3][:, width:]])
    small = pieces[Piece.S]
    mine = lax.dynamic_slice_in_dim(small[:6], me * (dim // shards), dim // shards, 1)
    rest = small[6:9].reshape(-1)
    return (
        have.output,
        have.input_grad,
        mine[0],
        mine[1],
        jnp.transpose(qkv_grad, (1, 0, 2)),
        rest[: 2 * width].reshape(2, width),
        out_grad.T,
        mine[2],
        mine[3],
        mine[4],
        up_grad,
        rest[2 * width :],
        down_grad.T,
        mine[5],
    )


def solution(mesh):
    in_specs = (
        P(DP, None),
        P(DP, None),
        P(DP, None),
        P(),
        P(),
        P(None, None, TENSOR),
        P(None, TENSOR),
        P(TENSOR, None),
        P(),
        P(),
        P(),
        P(None, TENSOR),
        P(TENSOR),
        P(TENSOR, None),
        P(),
    )
    out_specs = (
        P(DP, None),
        P(DP, None),
        P(DP),
        P(DP),
        P(DP, None, TENSOR),
        P(None, TENSOR),
        P(TENSOR, DP),
        P(DP),
        P(DP),
        P(DP),
        P(DP, TENSOR),
        P(TENSOR),
        P(TENSOR, DP),
        P(DP),
    )
    return jax.shard_map(
        functools.partial(per_device, mesh.shape[DP]),
        mesh=mesh,
        in_specs=in_specs,
        out_specs=out_specs,
        check_vma=False,
    )
```
